512 devices in a mesh: dp: 8 (over z), seq: 64 (over y, x, core).
Axes of the slice: x: 4, y: 8, z: 8, core: 2. Of those that a mesh axis runs over, the one named last changes fastest.
Arguments:
- tokens: bfloat16 [8, 32, 64, 2, 1024], P('dp', None, 'seq'), may hold values from -6 to 6
- text_weight: bfloat16 [1024, 1024], replicated, may hold values from -0.1875 to 0.1875
- conv_kernel: bfloat16 [31, 1024], replicated, may hold values from -1.5 to 1.5
- frame_token: int32 [8, 12288], P('dp', 'seq'), may hold values from 0 to 4095, as said below
- seg_before: int32 [8, 12288], P('dp', 'seq'), may hold values from 0 to 15, as said below
- seg_after: int32 [8, 12288], P('dp', 'seq'), may hold values from 0 to 15, as said below
- cotangent: bfloat16 [8, 12288, 1024], P('dp', 'seq'), may hold values from -0.01171875 to 0.01171875
Outputs:
- frames_out: bfloat16 [8, 12288, 1024], P('dp', 'seq')
- weight_grad: float32 [1024, 1024], P('seq')
The draws below stay inside these ranges and needn't reach their ends.
Inputs may be any that keep to these rules, and one draw needn't show every extreme that they name: Token t of a shard is repeated by a run of 2 or 4 consecutive frames; the runs follow the token order and fill the shard's 12288 frames exactly, so frame_token never falls along the frames. Packed segments are runs of whole tokens; seg_before is the number of frames of the frame's segment before it, or (30)/2 where that number is larger. seg_after is the number of frames of the frame's segment after it, or (30)/2 where that number is larger.
All inputs are finite; a program needn't handle non-finite values.
Results may differ from the reference program's by a relative error of at most 0.0057.
Values may be sent and summed in bfloat16 or wider, within the bound.
No kernel may reach another device: no remote copies, remote signals or barrier semaphores. Data moves between devices by JAX's collectives and lax.ppermute only.
A program may use at most 64 MiB of HBM per device.

```python
import jax
import jax.numpy as jnp
from jax import lax

D = 1024
KER = 31
TB = 2
GROUPS = 8
LANES = 64
SLOTS = 32
TOKENS = 4096
FRAMES = 12288


def shared_layout(key):

    def one_group(group_key):
        sub_keys = jax.random.split(group_key, 3)
        region = jnp.repeat(jax.random.randint(sub_keys[0], (TOKENS // 64,), 0, 2), 64)
        jitter = jax.random.permutation(sub_keys[1], TOKENS)
        ranking_score = region * TOKENS + jitter
        ranking = jnp.argsort(ranking_score)
        token_index = jnp.arange(TOKENS, dtype=jnp.int32)
        position = jnp.zeros((TOKENS,), jnp.int32).at[ranking].set(token_index)
        duration = 2 + 2 * (position >= TOKENS // 2).astype(jnp.int32)
        run_ends = jnp.cumsum(duration).astype(jnp.int32)
        begins = run_ends - duration
        frame_tok = jnp.repeat(token_index, duration, total_repeat_length=FRAMES).astype(jnp.int32)
        seg_flags = jax.random.randint(sub_keys[2], (TOKENS,), 0, 48) == 0
        seg_flags = seg_flags.at[1:16].set(False)
        seg_flags = seg_flags.at[0].set(True)
        seg_first = lax.cummax(jnp.where(seg_flags, token_index, 0))
        next_flag = lax.cummin(jnp.where(seg_flags, token_index, TOKENS), reverse=True)
        next_first = jnp.concatenate([next_flag[1:], jnp.array([TOKENS], jnp.int32)])
        begins_ext = jnp.concatenate([begins, jnp.array([FRAMES], jnp.int32)])
        first_frame = begins[seg_first][frame_tok]
        last_frame = begins_ext[next_first][frame_tok] - 1
        frame_index = jnp.arange(FRAMES, dtype=jnp.int32)
        before = jnp.minimum(frame_index - first_frame, KER // 2)
        after = jnp.minimum(last_frame - frame_index, KER // 2)
        return (frame_tok, before, after)
    return jax.vmap(one_group)(jax.random.split(key, GROUPS))


def draw_frame_token(key, part):
    return shared_layout(key)[0]


def draw_seg_before(key, part):
    return shared_layout(key)[1]


def draw_seg_after(key, part):
    return shared_layout(key)[2]


def block_scale(key, dims, shards, smallest, high):
    gain = 1.0
    for dim, shards_of in shards:
        heights = jax.random.uniform(jax.random.fold_in(jax.random.fold_in(key, 6), dim), (shards_of,), jnp.float32, smallest / len(shards), high / len(shards))
        gain = gain * jnp.repeat(jnp.exp(heights), dims[dim] // shards_of).reshape((-1,) + (1,) * (len(dims) - 1 - dim))
    return gain


def bell_draw(own_key, extent, scale, most, cuts=(), kind=jnp.bfloat16):
    loudness = block_scale(own_key, extent, cuts, -0.22, 0.18) if cuts else 1.0
    result = jax.random.normal(own_key, extent, jnp.float32) * scale * loudness
    return jnp.minimum(jnp.maximum(result, -most), most).astype(kind)


def setup_inputs(seed: int = 0) -> dict:
    streams_of = jax.random.split(jax.random.key(seed), 8)
    tokens = bell_draw(streams_of[0], (GROUPS, SLOTS, LANES, TB, D), 1.0, 6.0, ((0, 8), (2, 64)))
    text_weight = bell_draw(streams_of[1], (D, D), D ** -0.5, 0.1875)
    conv_kernel = bell_draw(streams_of[2], (KER, D), 0.25, 1.5)
    frame_token = draw_frame_token(jax.random.fold_in(streams_of[7], 71), 0)
    seg_before = draw_seg_before(jax.random.fold_in(streams_of[7], 71), 0)
    seg_after = draw_seg_after(jax.random.fold_in(streams_of[7], 71), 0)
    cotangent = bell_draw(streams_of[6], (GROUPS, FRAMES, D), (0.33 / (GROUPS * TOKENS) ** 0.5), 0.01171875, ((0, 8), (1, 64)))
    return dict(tokens=tokens, text_weight=text_weight, conv_kernel=conv_kernel, frame_token=frame_token, seg_before=seg_before, seg_after=seg_after, cotangent=cotangent)


def rms_rows(rows):
    wide = rows.astype(jnp.float32)
    scale = lax.rsqrt(lax.optimization_barrier(jnp.mean(wide * wide, axis=-1, keepdims=True)) + 1e-06)
    return (wide * scale).astype(jnp.bfloat16)

def depthwise(padded, kernel, low_len, high_len, direction, frame_count):
    half_span = kernel.shape[0] // 2
    taps = kernel.astype(jnp.float32)
    accumulated = jnp.zeros((frame_count, kernel.shape[1]), jnp.float32)
    for shift_by in range(-half_span, half_span + 1):
        offset = direction * shift_by
        shifted = padded[half_span + offset:half_span + offset + frame_count].astype(jnp.float32)
        inside = (shift_by >= -low_len) & (shift_by <= high_len)
        accumulated = accumulated + jnp.where(inside[:, None], taps[shift_by + half_span][None, :] * shifted, 0.0)
    return accumulated

def reference(tokens, text_weight, conv_kernel, frame_token, seg_before, seg_after, cotangent):
    half_span = KER // 2
    flat_tokens = tokens.reshape(GROUPS, TOKENS, D)

    def one_group(packed):
        group_tokens, group_frames, group_back, group_ahead, group_cot = packed
        normed = rms_rows(group_tokens)
        text_rows = jnp.dot(normed, text_weight, preferred_element_type=jnp.float32).astype(jnp.bfloat16)
        upsampled = jnp.take(text_rows, group_frames, axis=0)
        padded = jnp.pad(upsampled, ((half_span, half_span), (0, 0)))
        conv_out = depthwise(padded, conv_kernel, group_back, group_ahead, 1, FRAMES)
        frames_out = (upsampled.astype(jnp.float32) + conv_out).astype(jnp.bfloat16)
        grad_pad = jnp.pad(group_cot, ((half_span, half_span), (0, 0)))
        back_mix = depthwise(grad_pad, conv_kernel, group_ahead, group_back, -1, FRAMES)
        frame_grad = (group_cot.astype(jnp.float32) + back_mix).astype(jnp.bfloat16)
        token_grad = jax.ops.segment_sum(frame_grad.astype(jnp.float32), group_frames, num_segments=TOKENS)
        grad_part = jnp.dot(normed.astype(jnp.float32).T, token_grad, precision=lax.Precision.HIGHEST)
        return (frames_out, grad_part)
    frames_out, grad_parts = lax.map(one_group, (flat_tokens, frame_token, seg_before, seg_after, cotangent))
    return (frames_out, lax.optimization_barrier(jnp.sum(grad_parts, axis=0)))
```

```python
import jax
import jax.numpy as jnp
from jax import lax
from jax.sharding import PartitionSpec as P

LANE_GROUP = 8
SPLIT = 64


def rms_rows(rows):
    wide = rows.astype(jnp.float32)
    scale = lax.rsqrt(jnp.mean(wide * wide, axis=-1, keepdims=True) + 1e-06)
    return (wide * scale).astype(jnp.bfloat16)


def depthwise(padded, kernel, low_len, high_len, direction, frame_count):
    half_span = kernel.shape[0] // 2
    taps = kernel.astype(jnp.float32)
    accumulated = jnp.zeros((frame_count, kernel.shape[1]), jnp.float32)
    for shift_by in range(-half_span, half_span + 1):
        offset = direction * shift_by
        shifted = padded[half_span + offset : half_span + offset + frame_count].astype(jnp.float32)
        inside = (shift_by >= -low_len) & (shift_by <= high_len)
        accumulated = accumulated + jnp.where(
            inside[:, None], taps[shift_by + half_span][None, :] * shifted, 0.0
        )
    return accumulated


def split_whole(values):
    return (values // SPLIT).astype(jnp.bfloat16), (values % SPLIT).astype(jnp.bfloat16)


def join_whole(high, low):
    return high.astype(jnp.int32) * SPLIT + low.astype(jnp.int32)


def with_tokens(frames, toks):
    high, low = split_whole(toks)
    width = frames.shape[1]
    row = jnp.concatenate([high, low, jnp.zeros((width - 2 * toks.shape[0],), jnp.bfloat16)])
    return jnp.concatenate([frames, row[None]], axis=0)


def apart(rim):
    span = rim.shape[0] - 1
    return rim[:span], join_whole(rim[span, :span], rim[span, span : 2 * span])


def all_to_all(blocks, axis, groups=None):
    return lax.all_to_all(
        blocks, axis, split_axis=0, concat_axis=0, tiled=True, axis_index_groups=groups
    )


def body(tokens, text_weight, conv_kernel, frame_token, seg_before, seg_after, cotangent):
    peers = lax.axis_size("seq")
    shards = lax.axis_size("dp")
    rank = lax.axis_index("seq")
    slots, block_rows, width = tokens.shape[1], tokens.shape[3], tokens.shape[4]
    half_span = conv_kernel.shape[0] // 2
    groups = peers // LANE_GROUP
    columns = width // LANE_GROUP
    out_rows = width // peers
    f32, bf16 = jnp.float32, jnp.bfloat16

    grad_in = cotangent[0]
    frame_count = grad_in.shape[0]
    toks = frame_token[0]
    tail = with_tokens(grad_in[frame_count - half_span :], toks[frame_count - half_span :])
    head = with_tokens(grad_in[:half_span], toks[:half_span])
    right = [(i, i + 1) for i in range(peers - 1)]
    left = [(i + 1, i) for i in range(peers - 1)]
    before, toks_before = apart(lax.ppermute(tail, "seq", right))
    after, toks_after = apart(lax.ppermute(head, "seq", left))

    normed = rms_rows(tokens.reshape(slots * block_rows, width))
    text_rows = jnp.dot(normed, text_weight, preferred_element_type=f32).astype(bf16)
    members = [[g * LANE_GROUP + i for i in range(LANE_GROUP)] for g in range(groups)]
    group_normed = all_to_all(
        jnp.broadcast_to(normed[None], (LANE_GROUP,) + normed.shape), "seq", members
    )

    seg_back, seg_ahead = seg_before[0], seg_after[0]
    back_mix = depthwise(
        jnp.concatenate([before, grad_in, after]), conv_kernel, seg_ahead, seg_back, -1, frame_count
    )
    frame_grad = (grad_in.astype(f32) + back_mix).astype(bf16)
    frame_grad = lax.optimization_barrier(frame_grad)

    all_toks = jnp.concatenate([toks_before, toks, toks_after])
    column = all_toks // block_rows % peers * block_rows + all_toks % block_rows
    onehot = (
        column[:, None] == jnp.arange(peers * block_rows, dtype=jnp.int32)[None, :]
    ).astype(bf16)
    sums = jnp.einsum(
        "fc,fd->cd",
        onehot[half_span : half_span + frame_count],
        frame_grad,
        preferred_element_type=f32,
    ).astype(bf16)
    sums = sums.reshape(groups, LANE_GROUP, block_rows, LANE_GROUP, columns)
    sums = sums.transpose(0, 3, 2, 1, 4).reshape(peers, block_rows, LANE_GROUP * columns)
    first_block = toks_before[0] // block_rows
    high, low = split_whole(first_block)
    note = jnp.where(jnp.arange(128) == 0, high, jnp.where(jnp.arange(128) == 1, low, 0)).astype(bf16)
    note = jnp.broadcast_to(note, (peers, block_rows, 128))
    returned = all_to_all(jnp.concatenate([sums, note], axis=2), "seq")

    starts = join_whole(returned[:, 0, width], returned[:, 0, width + 1])
    lanes = rank // LANE_GROUP * LANE_GROUP + jnp.arange(LANE_GROUP, dtype=jnp.int32)
    wanted = starts[None] + jnp.mod(lanes[:, None] - starts[None], peers)
    slot_of = wanted // peers
    owners = (
        slot_of[:, None, :] == jnp.arange(slots, dtype=jnp.int32)[None, :, None]
    ).astype(bf16)
    gathered = returned[:, :, :width].reshape(peers, block_rows, LANE_GROUP, columns)
    token_grad = jnp.einsum("lsk,krlc->lsrc", owners, gathered, preferred_element_type=f32)
    token_grad = token_grad.reshape(LANE_GROUP * slots * block_rows, columns)
    upper = token_grad.astype(bf16)
    lower = (token_grad - upper.astype(f32)).astype(bf16)
    group_normed = group_normed.reshape(LANE_GROUP * slots * block_rows, width)
    product = jnp.einsum(
        "tn,tc->nc", group_normed, jnp.concatenate([upper, lower], axis=1), preferred_element_type=f32
    )
    partial_grad = (product[:, :columns] + product[:, columns:]).astype(bf16)

    my_slots = starts + jnp.mod(rank - starts, peers)
    my_slots = jnp.minimum(my_slots // peers, slots - 1)
    send_text = text_rows.reshape(slots, block_rows, width)[my_slots]
    arrived = all_to_all(
        jnp.concatenate([partial_grad.reshape(peers, block_rows, width), send_text], axis=1), "seq"
    )

    rows_mine = arrived[:, :block_rows].reshape(groups, LANE_GROUP, out_rows, columns)
    rows_mine = jnp.sum(rows_mine.astype(f32), axis=0)
    rows_mine = rows_mine.transpose(1, 0, 2).reshape(out_rows, width).astype(bf16)
    shares = all_to_all(jnp.broadcast_to(rows_mine[None], (shards,) + rows_mine.shape), "dp")
    summed = jnp.sum(shares.astype(f32), axis=0)

    upsampled = jnp.dot(
        onehot,
        arrived[:, block_rows:].reshape(peers * block_rows, width),
        preferred_element_type=f32,
    ).astype(bf16)
    upsampled = lax.optimization_barrier(upsampled)
    conv_out = depthwise(upsampled, conv_kernel, seg_back, seg_ahead, 1, frame_count)
    own = upsampled[half_span : half_span + frame_count]
    frames_out = (own.astype(f32) + conv_out).astype(bf16)
    return (frames_out[None], summed)


def solution(mesh):
    in_specs = (
        P("dp", None, "seq", None, None),
        P(),
        P(),
        P("dp", "seq"),
        P("dp", "seq"),
        P("dp", "seq"),
        P("dp", "seq", None),
    )
    out_specs = (P("dp", "seq", None), P("seq", None))
    return jax.shard_map(body, mesh=mesh, in_specs=in_specs, out_specs=out_specs, check_vma=False)
```

```python
import jax
import jax.numpy as jnp
from jax import lax
from jax.experimental import pallas as pl
from jax.experimental.pallas import tpu as pltpu
from jax.sharding import PartitionSpec as P

EDGE = 16
SPLIT_BITS = 6
LOW_AT = 256
ROWS = 8
LANE = 128
MEMBERS = 8
HALVES = ROWS // MEMBERS
F32, BF16, I32 = jnp.float32, jnp.bfloat16, jnp.int32


def rms_rows(rows):
    wide = rows.astype(F32)
    scale = lax.rsqrt(jnp.mean(wide * wide, axis=-1, keepdims=True) + 1e-06)
    return (wide * scale).astype(BF16)


def rim_kernel(
    cot_any, toks_any, back_any, ahead_any, kernel_any,
    tail_ref, head_ref, cot_ref, toks_ref, back_ref, ahead_ref, kernel_ref, note, sems,
):
    pairs = (
        (cot_any, cot_ref), (toks_any, toks_ref), (back_any, back_ref), (ahead_any, ahead_ref),
        (kernel_any, kernel_ref),
    )
    moves = [
        pltpu.make_async_copy(source, target, sems.at[index])
        for index, (source, target) in enumerate(pairs)
    ]
    for move in moves:
        move.start()
    note[...] = jnp.zeros_like(note)
    for move in moves:
        move.wait()
    frame_count = toks_ref.shape[1]
    toks = toks_ref[...]
    note[:1, :frame_count] = (toks >> SPLIT_BITS).astype(F32)
    note[:1, LOW_AT : LOW_AT + frame_count] = (toks & (1 << SPLIT_BITS) - 1).astype(F32)
    line = lax.broadcasted_iota(I32, tail_ref.shape, 0)
    row = note[:1]
    last = cot_ref[frame_count - EDGE :].astype(F32)
    first = cot_ref[:EDGE].astype(F32)
    tail_ref[...] = jnp.where(line == 0, row, last).astype(BF16)
    head_ref[...] = jnp.where(line == EDGE - 1, row, first).astype(BF16)


def norm_kernel(own_ref, normed_ref):
    normed_ref[...] = rms_rows(own_ref[...])


def text_kernel(normed_ref, weight_ref, text_ref):
    text_ref[...] = jnp.dot(
        normed_ref[...], weight_ref[...], preferred_element_type=F32
    ).astype(BF16)


def down_rows(row, count):
    square = (count, count)
    here = lax.broadcasted_iota(jnp.int32, square, 0) == lax.broadcasted_iota(jnp.int32, square, 1)
    diagonal = jnp.where(here, row.astype(F32), 0.0).astype(BF16)
    return jnp.dot(diagonal, jnp.ones((count, LANE), BF16), preferred_element_type=F32)


def prepare(shifted, taps, low, high, kernel_ref, low_ref, high_ref, frame_count):
    low[...] = down_rows(low_ref[...], frame_count)
    high[...] = down_rows(high_ref[...], frame_count)
    wide = kernel_ref[...].astype(F32)
    for tap in range(wide.shape[0]):
        taps[tap] = jnp.broadcast_to(wide[tap : tap + 1], (ROWS, wide.shape[1]))
    rows, width = shifted.shape[1], shifted.shape[2]

    def shift(block, _):
        lanes = pl.ds(pl.multiple_of(block * LANE, LANE), LANE)
        window = shifted[0, :, lanes]
        for by in range(1, ROWS):
            shifted[by, :, lanes] = pltpu.roll(window, rows - by, 0)
        return 0

    lax.fori_loop(0, width // LANE, shift, 0)


def convolve(shifted, taps, low, high, direction, out_ref, frame_count):
    half_span = taps.shape[0] // 2
    blocks = shifted.shape[2] // LANE
    step = 2 * ROWS

    def chunk(index, _):
        base = pl.multiple_of(index * step, step)
        totals = [[None] * blocks for _ in range(2)]
        lows = [low[pl.ds(base + part * ROWS, ROWS), :] for part in range(2)]
        highs = [high[pl.ds(base + part * ROWS, ROWS), :] for part in range(2)]
        order = [0] + [k for far in range(1, half_span + 1) for k in (-far, far)]
        for shift_by in order:
            row = EDGE + direction * shift_by
            by, first = row % ROWS, row // ROWS * ROWS
            if shift_by < 0:
                inside = [value >= float(-shift_by) for value in lows]
            else:
                inside = [value >= float(shift_by) for value in highs]
            for block in range(blocks):
                lanes = slice(block * LANE, (block + 1) * LANE)
                tap = taps[shift_by + half_span, :, lanes]
                for part in range(2):
                    values = shifted[by, pl.ds(base + first + part * ROWS, ROWS), lanes]
                    term = tap * values
                    if shift_by == 0:
                        totals[part][block] = values + term
                    else:
                        totals[part][block] += jnp.where(inside[part], term, 0.0)
        for block in range(blocks):
            lanes = slice(block * LANE, (block + 1) * LANE)
            both = jnp.concatenate([totals[0][block], totals[1][block]], axis=0)
            out_ref[pl.ds(base, step), lanes] = both.astype(BF16)
        return 0

    lax.fori_loop(0, frame_count // step, chunk, 0)


def grad_kernel(
    cot_ref, before_ref, after_ref, kernel_ref, back_ref, ahead_ref, toks_ref, out_ref,
    shifted, taps, low, high, frame_grad,
):
    frame_count, width = cot_ref.shape
    shifted[0, :EDGE, :] = before_ref[...].astype(F32)
    shifted[0, EDGE : EDGE + frame_count, :] = cot_ref[...].astype(F32)
    shifted[0, EDGE + frame_count :, :] = after_ref[...].astype(F32)
    prepare(shifted, taps, low, high, kernel_ref, ahead_ref, back_ref, frame_count)
    convolve(shifted, taps, low, high, -1, frame_grad, frame_count)
    peers = out_ref.shape[0]
    columns = 2 * peers
    chosen = toks_ref[...] & columns - 1
    onehot = lax.broadcasted_iota(I32, (columns, frame_count), 0) == chosen
    sums = jnp.dot(
        jnp.where(onehot, 1.0, 0.0).astype(BF16), frame_grad[...], preferred_element_type=F32
    )
    at = note_at(frame_count) // LANE * LANE
    line = lax.broadcasted_iota(I32, (ROWS, LANE), 0)
    upper = before_ref[:, at : at + LANE].astype(F32)[:1]
    lower = before_ref[:, LOW_AT + at : LOW_AT + at + LANE].astype(F32)[:1]
    note = jnp.where(line < ROWS // 2, upper, lower).astype(BF16)
    for peer in range(peers):
        group, part = peer // MEMBERS, peer % MEMBERS
        rows = slice(group * 2 * MEMBERS, (group + 1) * 2 * MEMBERS)
        first = part * HALVES * LANE
        block = [
            sums[rows, first + half * LANE : first + (half + 1) * LANE] for half in range(HALVES)
        ]
        out_ref[peer, :EDGE, :] = jnp.concatenate(block, axis=0).astype(BF16)
        out_ref[peer, EDGE : EDGE + ROWS, :] = note


def note_at(frame_count):
    return frame_count - EDGE + 1


def product_kernel(
    rank_ref, returned_ref, text_ref, *refs, slots, block_rows, frame_count
):
    *pieces, out_ref, marks, normed, spread = refs
    peers = returned_ref.shape[0]
    rows, width = text_ref.shape
    terms = peers * EDGE
    rank = rank_ref[0]
    at = 0
    for piece in pieces:
        normed[at : at + piece.shape[0]] = piece[...]
        at += piece.shape[0]

    note = returned_ref[:, EDGE : EDGE + ROWS, :].astype(F32).reshape(peers * ROWS, LANE)
    line = lax.broadcasted_iota(I32, (LANE, LANE), 0)
    chosen = jnp.where(line == note_at(frame_count) % LANE, 1.0, 0.0).astype(BF16)
    marks[...] = jnp.dot(note.astype(BF16), chosen, preferred_element_type=F32)
    upper = marks[pl.ds(0, peers, stride=ROWS), :]
    lower = marks[pl.ds(ROWS // 2, peers, stride=ROWS), :]
    shape = (peers, terms)
    here = lax.broadcasted_iota(I32, shape, 1) // EDGE == lax.broadcasted_iota(I32, shape, 0)

    def along(values):
        wide = jnp.concatenate([values] * (terms // LANE), axis=1)
        wide = jnp.where(here, wide, 0.0).astype(BF16)
        ones = jnp.ones((ROWS, peers), BF16)
        return jnp.dot(ones, wide, preferred_element_type=F32)[:1]

    def block_of(upper, lower):
        return ((upper.astype(I32) << SPLIT_BITS) + lower.astype(I32)) // block_rows

    def slot_of(starts, lane):
        return (starts + (lane - starts & peers - 1)) // peers

    starts = block_of(along(upper), along(lower))
    term = lax.broadcasted_iota(I32, (1, terms), 1)
    member = term // block_rows & MEMBERS - 1
    half = term // (block_rows * MEMBERS) & HALVES - 1
    slot = slot_of(starts, rank // MEMBERS * MEMBERS + member)
    total = MEMBERS * rows
    chips = MEMBERS // 2
    away = ((rank & MEMBERS - 1) // 2 - member // 2) & chips - 1
    target = half * total + ((rank ^ member) & 1) * chips * rows + away * rows
    target = target + slot * block_rows + (term & block_rows - 1)
    target = jnp.where(slot < slots, target, -1)
    onehot = lax.broadcasted_iota(I32, (HALVES * total, terms), 0) == target
    token_grad = jnp.dot(
        jnp.where(onehot, 1.0, 0.0).astype(BF16),
        returned_ref[:, :EDGE, :].reshape(terms, LANE),
        preferred_element_type=F32,
    )
    for part in range(HALVES):
        grad = token_grad[part * total : (part + 1) * total]
        first = grad.astype(BF16)
        second = (grad - first.astype(F32)).astype(BF16)
        product = lax.dot_general(
            normed[...],
            jnp.concatenate([first, second], axis=1),
            (((0,), (0,)), ((), ())),
            preferred_element_type=F32,
        )
        product = (product[:, :LANE] + product[:, LANE:]).astype(BF16)
        out_ref[:, EDGE * (part + 1) : EDGE * (part + 2), :] = product.reshape(peers, EDGE, LANE)

    mine = slot_of(block_of(upper, lower), rank)[:, :rows]
    mine = jnp.minimum(mine, slots - 1) * block_rows
    column = lax.broadcasted_iota(I32, (peers, rows), 1)
    for row in range(block_rows):
        picks = jnp.where(column == mine + row, 1.0, 0.0).astype(BF16)
        picked = jnp.dot(picks, text_ref[...], preferred_element_type=F32)
        for part in range(ROWS):
            spread[pl.ds(row * ROWS + part, peers, stride=EDGE), :] = picked[
                :, part * LANE : (part + 1) * LANE
            ]
    out_ref[:, :EDGE, :] = spread[...].astype(BF16).reshape(peers, EDGE, LANE)


def share_kernel(arrived_ref, copies_ref):
    peers = arrived_ref.shape[0]
    for part in range(MEMBERS):
        for half in range(HALVES):
            total = jnp.zeros((EDGE, LANE), F32)
            for group in range(peers // MEMBERS):
                total += arrived_ref[
                    group * MEMBERS + part, EDGE * (half + 1) : EDGE * (half + 2), :
                ].astype(F32)
            first = (part * HALVES + half) * LANE
            for copy in range(copies_ref.shape[0]):
                copies_ref[copy, :, first : first + LANE] = total.astype(BF16)


def frame_kernel(
    arrived_ref, toks_ref, kernel_ref, back_ref, ahead_ref, out_ref, shifted, taps, low, high, spread
):
    frame_count = out_ref.shape[0]
    rows = shifted.shape[1]
    columns = 2 * arrived_ref.shape[0]
    spread[...] = arrived_ref[:, :EDGE, :].astype(F32).reshape(columns * ROWS, LANE)
    chosen = down_rows(toks_ref[...] & columns - 1, rows)
    onehot = chosen == lax.broadcasted_iota(I32, (rows, columns), 1).astype(F32)
    onehot = jnp.where(onehot, 1.0, 0.0).astype(BF16)
    for part in range(ROWS):
        shifted[0, :, part * LANE : (part + 1) * LANE] = jnp.dot(
            onehot,
            spread[pl.ds(part, columns, stride=ROWS), :].astype(BF16),
            preferred_element_type=F32,
        )
    prepare(shifted, taps, low, high, kernel_ref, back_ref, ahead_ref, frame_count)
    convolve(shifted, taps, low, high, 1, out_ref, frame_count)


SMALL, LARGE = pl.BlockSpec(memory_space=pltpu.SMEM), pl.BlockSpec(memory_space=pltpu.VMEM)


def call(kernel, outs, scratch, flops, moved, ins=None, mib=16):
    options = {} if ins is None else {"in_specs": ins}
    return pl.pallas_call(
        kernel,
        out_shape=outs,
        scratch_shapes=scratch,
        compiler_params=pltpu.CompilerParams(vmem_limit_bytes=mib * 1024 * 1024),
        cost_estimate=pl.CostEstimate(flops=flops, bytes_accessed=moved, transcendentals=0),
        **options,
    )


def all_to_all(blocks, axis):
    return lax.all_to_all(blocks, axis, split_axis=0, concat_axis=0, tiled=True)


def body(tokens, text_weight, conv_kernel, frame_token, seg_before, seg_after, cotangent):
    peers = lax.axis_size("seq")
    shards = lax.axis_size("dp")
    rank = lax.axis_index("seq")
    slots, block_rows, width = tokens.shape[1], tokens.shape[3], tokens.shape[4]
    half_span = conv_kernel.shape[0] // 2
    frame_count = cotangent.shape[1]
    own_rows = slots * block_rows
    cot = cotangent[0]
    rank_word = rank[None]

    rim = jax.ShapeDtypeStruct((EDGE, width), BF16)
    line = jax.ShapeDtypeStruct((1, frame_count), I32)
    given = [
        pltpu.with_memory_space_constraint(array, pltpu.HBM)
        for array in (cot, frame_token, seg_before, seg_after, conv_kernel)
    ]
    tail, head, cot, toks, back, ahead, taps = call(
        rim_kernel,
        [rim, rim, jax.ShapeDtypeStruct(cot.shape, BF16), line, line, line]
        + [jax.ShapeDtypeStruct(conv_kernel.shape, BF16)],
        [pltpu.VMEM((ROWS, width), F32), pltpu.SemaphoreType.DMA((len(given),))],
        8 * EDGE * width,
        4 * frame_count * width,
        [pl.BlockSpec(memory_space=pltpu.HBM)] * len(given),
        mib=4,
    )(*given)
    before = lax.ppermute(tail, "seq", [(i, i + 1) for i in range(peers - 1)])
    after = lax.ppermute(head, "seq", [(i + 1, i) for i in range(peers - 1)])
    normed = call(
        norm_kernel,
        jax.ShapeDtypeStruct((own_rows, width), BF16),
        [],
        8 * own_rows * width,
        4 * own_rows * width,
        mib=4,
    )(tokens.reshape(own_rows, width))
    text_rows = call(
        text_kernel,
        jax.ShapeDtypeStruct((own_rows, width), BF16),
        [],
        2 * own_rows * width * width,
        2 * width * width,
        mib=8,
    )(normed, text_weight)

    def hop(count):
        path = [(i, i // MEMBERS * MEMBERS + (i + 2 * count) % MEMBERS) for i in range(peers)]
        return lax.ppermute(normed, "seq", path)

    pieces = [normed] + [hop(count) for count in range(1, MEMBERS // 2)]

    scratch = [
        pltpu.VMEM((ROWS, frame_count + 2 * EDGE, width), F32),
        pltpu.VMEM((conv_kernel.shape[0], ROWS, width), F32),
        pltpu.VMEM((frame_count, LANE), F32),
        pltpu.VMEM((frame_count, LANE), F32),
    ]
    work = 12 * conv_kernel.shape[0] * frame_count * width
    packed = call(
        grad_kernel,
        jax.ShapeDtypeStruct((peers, EDGE + ROWS, LANE), BF16),
        scratch + [pltpu.VMEM((frame_count, width), BF16)],
        work,
        4 * frame_count * width,
    )(cot, before, after, taps, back, ahead, toks)
    returned = all_to_all(packed, "seq")
    pieces.append(
        lax.ppermute(jnp.concatenate(pieces), "seq", [(i, i ^ 1) for i in range(peers)])
    )

    def toks_of(note):
        note = note.astype(I32)
        return (note[:frame_count] << SPLIT_BITS) + note[LOW_AT : LOW_AT + frame_count]

    none = jnp.zeros((1,), I32)
    all_toks = jnp.concatenate(
        [
            none,
            toks_of(before[0])[frame_count - half_span :],
            toks[0],
            toks_of(after[EDGE - 1])[:half_span],
            none,
        ]
    )[None]
    product = call(
        lambda *refs: product_kernel(
            *refs, slots=slots, block_rows=block_rows, frame_count=frame_count
        ),
        jax.ShapeDtypeStruct((peers, EDGE * (1 + HALVES), LANE), BF16),
        [
            pltpu.VMEM((peers * ROWS, LANE), F32),
            pltpu.VMEM((MEMBERS * own_rows, width), BF16),
            pltpu.VMEM((peers * EDGE, LANE), F32),
        ],
        4 * MEMBERS * own_rows * width * LANE * HALVES,
        4 * MEMBERS * own_rows * width,
        [SMALL] + [LARGE] * (2 + len(pieces)),
        24,
    )(rank_word, returned, text_rows, *pieces)
    arrived = all_to_all(product, "seq")

    copies = call(
        share_kernel,
        jax.ShapeDtypeStruct((shards, width // peers, width), BF16),
        [],
        peers * EDGE * HALVES * LANE,
        peers * EDGE * HALVES * LANE,
    )(arrived)
    shares = all_to_all(copies, "dp")
    summed = jnp.sum(shares.astype(F32), axis=0)

    frames_out = call(
        frame_kernel,
        jax.ShapeDtypeStruct((frame_count, width), BF16),
        scratch + [pltpu.VMEM((peers * EDGE, LANE), F32)],
        work,
        4 * frame_count * width,
    )(arrived, all_toks, taps, back, ahead)
    return (frames_out[None], summed)


def solution(mesh):
    in_specs = (
        P("dp", None, "seq", None, None),
        P(),
        P(),
        P("dp", "seq"),
        P("dp", "seq"),
        P("dp", "seq"),
        P("dp", "seq", None),
    )
    out_specs = (P("dp", "seq", None), P("seq", None))
    return jax.shard_map(body, mesh=mesh, in_specs=in_specs, out_specs=out_specs, check_vma=False)
```

```python
import jax
import jax.numpy as jnp
from jax import lax
from jax.experimental import pallas as pl
from jax.experimental.pallas import tpu as pltpu
from jax.sharding import PartitionSpec as P

EDGE = 16
LEAD = 32
SPLIT_BITS = 6
LOW_AT, BACK_AT, AHEAD_AT = 256, 512, 768
ROWS = 8
LANE = 128
MEMBERS = 8
HALVES = ROWS // MEMBERS
F32, BF16, I32 = jnp.float32, jnp.bfloat16, jnp.int32


def rms_rows(rows):
    wide = rows.astype(F32)
    scale = lax.rsqrt(jnp.mean(wide * wide, axis=-1, keepdims=True) + 1e-06)
    return (wide * scale).astype(BF16)


def rim_kernel(
    cot_any, toks_any, back_any, ahead_any, own_any,
    tail_ref, cot_ref, toks_ref, back_ref, ahead_ref, normed_ref, note, own, sems,
):
    pairs = (
        (cot_any, cot_ref), (toks_any, toks_ref), (back_any, back_ref), (ahead_any, ahead_ref),
        (own_any, own),
    )
    moves = [
        pltpu.make_async_copy(source, target, sems.at[index])
        for index, (source, target) in enumerate(pairs)
    ]
    for move in moves:
        move.start()
    note[...] = jnp.zeros_like(note)
    for move in moves:
        move.wait()
    frame_count = toks_ref.shape[1]
    toks = toks_ref[...]
    values = (toks >> SPLIT_BITS, toks & (1 << SPLIT_BITS) - 1, back_ref[...], ahead_ref[...])
    for at, value in zip((0, LOW_AT, BACK_AT, AHEAD_AT), values):
        note[:1, at : at + frame_count] = value.astype(F32)
    line = lax.broadcasted_iota(I32, tail_ref.shape, 0)
    last = cot_ref[frame_count - LEAD :].astype(F32)
    tail_ref[...] = jnp.where(line == 0, note[:1], last).astype(BF16)
    normed_ref[...] = rms_rows(own[...].astype(F32).reshape(normed_ref.shape))


def text_kernel(normed_ref, weight_ref, text_ref):
    text_ref[...] = jnp.dot(
        normed_ref[...], weight_ref[...], preferred_element_type=F32
    ).astype(BF16)


def down_rows(row, count):
    square = (count, count)
    here = lax.broadcasted_iota(jnp.int32, square, 0) == lax.broadcasted_iota(jnp.int32, square, 1)
    diagonal = jnp.where(here, row.astype(F32), 0.0).astype(BF16)
    return jnp.dot(diagonal, jnp.ones((count, LANE), BF16), preferred_element_type=F32)


def prepare(shifted, taps, kernel_far, kernel_here, sem):
    move = pltpu.make_async_copy(kernel_far, kernel_here, sem)
    move.start()
    rows, width = shifted.shape[1], shifted.shape[2]

    def shift(block, _):
        lanes = pl.ds(pl.multiple_of(block * LANE, LANE), LANE)
        window = shifted[0, :, lanes]
        for by in range(1, ROWS):
            shifted[by, :, lanes] = pltpu.roll(window, rows - by, 0)
        return 0

    lax.fori_loop(0, width // LANE, shift, 0)
    move.wait()
    wide = kernel_here[...].astype(F32)
    for tap in range(wide.shape[0]):
        taps[tap] = jnp.broadcast_to(wide[tap : tap + 1], (ROWS, width))


def convolve(shifted, taps, low, high, direction, first_row, out_ref, chunks):
    half_span = taps.shape[0] // 2
    blocks = shifted.shape[2] // LANE
    step = 2 * ROWS

    def chunk(index, _):
        base = pl.multiple_of(index * step, step)
        totals = [[None] * blocks for _ in range(2)]
        lows = [low[pl.ds(base + part * ROWS, ROWS), :] for part in range(2)]
        highs = [high[pl.ds(base + part * ROWS, ROWS), :] for part in range(2)]
        order = [0] + [k for far in range(1, half_span + 1) for k in (-far, far)]
        for shift_by in order:
            row = first_row + direction * shift_by
            by, first = row % ROWS, row // ROWS * ROWS
            if shift_by < 0:
                inside = [value >= float(-shift_by) for value in lows]
            else:
                inside = [value >= float(shift_by) for value in highs]
            for block in range(blocks):
                lanes = slice(block * LANE, (block + 1) * LANE)
                tap = taps[shift_by + half_span, :, lanes]
                for part in range(2):
                    values = shifted[by, pl.ds(base + first + part * ROWS, ROWS), lanes]
                    term = tap * values
                    if shift_by == 0:
                        totals[part][block] = values + term
                    else:
                        totals[part][block] += jnp.where(inside[part], term, 0.0)
        for block in range(blocks):
            lanes = slice(block * LANE, (block + 1) * LANE)
            both = jnp.concatenate([totals[0][block], totals[1][block]], axis=0)
            out_ref[pl.ds(base, step), lanes] = both.astype(BF16)
        return 0

    lax.fori_loop(0, chunks, chunk, 0)


def grad_kernel(
    rank_ref, cot_ref, before_ref, kernel_far, back_ref, ahead_ref, toks_ref, out_ref,
    shifted, taps, low, high, kernel_here, sem, frame_grad,
):
    frame_count, width = cot_ref.shape
    peers = out_ref.shape[0]
    columns = 2 * peers
    last = jnp.where(rank_ref[0] == peers - 1, 1, 0)
    shifted[0, :LEAD, :] = before_ref[...].astype(F32)
    shifted[0, LEAD : LEAD + frame_count, :] = cot_ref[...].astype(F32)
    shifted[0, LEAD + frame_count :, :] = jnp.zeros((EDGE, width), F32)
    count, half_span = frame_grad.shape[0], taps.shape[0] // 2
    shape = (count, frame_count)
    line, lane = lax.broadcasted_iota(I32, shape, 0), lax.broadcasted_iota(I32, shape, 1)
    ours, theirs = lane == line - half_span, lane == line - half_span + frame_count
    note = before_ref[:EDGE, :].astype(F32)[:1]

    def of_frames(their, own):
        chosen = jnp.where(ours, own.astype(F32), jnp.where(theirs, their, 0.0)).astype(BF16)
        ones = jnp.ones((frame_count, LANE), BF16)
        return jnp.dot(chosen, ones, preferred_element_type=F32)

    low[...] = of_frames(note[:, AHEAD_AT : AHEAD_AT + frame_count], ahead_ref[...])
    high[...] = of_frames(note[:, BACK_AT : BACK_AT + frame_count], back_ref[...])
    prepare(shifted, taps, kernel_far, kernel_here, sem)
    frame_grad[frame_count:] = jnp.zeros((EDGE, width), BF16)
    first_row = LEAD - half_span
    convolve(
        shifted, taps, low, high, -1, first_row, frame_grad, frame_count // EDGE + last
    )
    their = note[:, :frame_count] * float(1 << SPLIT_BITS) + note[:, LOW_AT : LOW_AT + frame_count]
    their = (their.astype(I32) & columns - 1).astype(F32)
    chosen = of_frames(their, toks_ref[...] & columns - 1)
    place = lax.broadcasted_iota(I32, chosen.shape, 0)
    end = frame_count + last * half_span
    spot = lax.broadcasted_iota(I32, chosen.shape, 1).astype(F32)
    onehot = jnp.where((chosen == spot) & (place < end), 1.0, 0.0).astype(BF16)
    sums = lax.dot_general(
        onehot, frame_grad[...], (((0,), (0,)), ((), ())), preferred_element_type=F32
    )
    at = note_at(frame_count) // LANE * LANE
    line = lax.broadcasted_iota(I32, (ROWS, LANE), 0) // 2
    own = toks_ref[:, :LANE]
    lines = (
        note[:, at : at + LANE],
        note[:, LOW_AT + at : LOW_AT + at + LANE],
        (own >> SPLIT_BITS).astype(F32),
        (own & (1 << SPLIT_BITS) - 1).astype(F32),
    )
    marks = jnp.zeros((ROWS, LANE), F32)
    for index, value in enumerate(lines):
        marks = jnp.where(line == index, value, marks)
    marks = marks.astype(BF16)
    for peer in range(peers):
        group, part = peer // MEMBERS, peer % MEMBERS
        rows = slice(group * 2 * MEMBERS, (group + 1) * 2 * MEMBERS)
        first = part * HALVES * LANE
        block = [
            sums[rows, first + half * LANE : first + (half + 1) * LANE] for half in range(HALVES)
        ]
        out_ref[peer, :EDGE, :] = jnp.concatenate(block, axis=0).astype(BF16)
        out_ref[peer, EDGE : EDGE + ROWS, :] = marks


def note_at(frame_count):
    return frame_count - EDGE + 1


def product_kernel(
    rank_ref, returned_ref, text_ref, same_far, other_ref, out_ref, marks, normed, spread, sem,
    *, slots, block_rows, frame_count,
):
    peers = returned_ref.shape[0]
    rows, width = text_ref.shape
    terms = peers * EDGE
    rank = rank_ref[0]
    move = pltpu.make_async_copy(same_far, normed, sem)
    move.start()

    note = returned_ref[:, EDGE : EDGE + ROWS, :].astype(F32).reshape(peers * ROWS, LANE)
    line = lax.broadcasted_iota(I32, (LANE, LANE), 0)
    chosen = jnp.where(line == note_at(frame_count) % LANE, 1.0, 0.0).astype(BF16)
    marks[...] = jnp.dot(note.astype(BF16), chosen, preferred_element_type=F32)
    upper = marks[pl.ds(0, peers, stride=ROWS), :]
    lower = marks[pl.ds(2, peers, stride=ROWS), :]
    shape = (peers, terms)
    here = lax.broadcasted_iota(I32, shape, 1) // EDGE == lax.broadcasted_iota(I32, shape, 0)

    def along(values):
        wide = jnp.concatenate([values] * (terms // LANE), axis=1)
        wide = jnp.where(here, wide, 0.0).astype(BF16)
        ones = jnp.ones((ROWS, peers), BF16)
        return jnp.dot(ones, wide, preferred_element_type=F32)[:1]

    def block_of(upper, lower):
        return ((upper.astype(I32) << SPLIT_BITS) + lower.astype(I32)) // block_rows

    def slot_of(starts, lane):
        return (starts + (lane - starts & peers - 1)) // peers

    starts = block_of(along(upper), along(lower))
    term = lax.broadcasted_iota(I32, (1, terms), 1)
    member = term // block_rows & MEMBERS - 1
    half = term // (block_rows * MEMBERS) & HALVES - 1
    slot = slot_of(starts, rank // MEMBERS * MEMBERS + member)
    total = MEMBERS * rows
    chips = MEMBERS // 2
    away = ((rank & MEMBERS - 1) // 2 - member // 2) & chips - 1
    target = half * total + ((rank ^ member) & 1) * chips * rows + away * rows
    target = target + slot * block_rows + (term & block_rows - 1)
    target = jnp.where(slot < slots, target, -1)
    onehot = lax.broadcasted_iota(I32, (HALVES * total, terms), 0) == target
    token_grad = jnp.dot(
        jnp.where(onehot, 1.0, 0.0).astype(BF16),
        returned_ref[:, :EDGE, :].reshape(terms, LANE),
        preferred_element_type=F32,
    )
    mine = slot_of(block_of(upper, lower), rank)[:, :rows]
    mine = jnp.minimum(mine, slots - 1) * block_rows
    column = lax.broadcasted_iota(I32, (peers, rows), 1)
    for row in range(block_rows):
        picks = jnp.where(column == mine + row, 1.0, 0.0).astype(BF16)
        picked = jnp.dot(picks, text_ref[...], preferred_element_type=F32)
        for part in range(ROWS):
            spread[pl.ds(row * ROWS + part, peers, stride=EDGE), :] = picked[
                :, part * LANE : (part + 1) * LANE
            ]
    out_ref[:, :EDGE, :] = spread[...].astype(BF16).reshape(peers, EDGE, LANE)

    move.wait()
    for part in range(HALVES):
        grad = token_grad[part * total : (part + 1) * total]
        first = grad.astype(BF16)
        second = (grad - first.astype(F32)).astype(BF16)
        both = jnp.concatenate([first, second], axis=1)
        product = jnp.zeros((width, 2 * LANE), F32)
        for index, ref in enumerate((normed, other_ref)):
            rows_of = slice(index * total // 2, (index + 1) * total // 2)
            product += lax.dot_general(
                ref[...], both[rows_of], (((0,), (0,)), ((), ())), preferred_element_type=F32
            )
        product = (product[:, :LANE] + product[:, LANE:]).astype(BF16)
        out_ref[:, EDGE * (part + 1) : EDGE * (part + 2), :] = product.reshape(peers, EDGE, LANE)


def share_kernel(arrived_ref, copies_ref):
    peers = arrived_ref.shape[0]
    for part in range(MEMBERS):
        for half in range(HALVES):
            total = jnp.zeros((EDGE, LANE), F32)
            for group in range(peers // MEMBERS):
                total += arrived_ref[
                    group * MEMBERS + part, EDGE * (half + 1) : EDGE * (half + 2), :
                ].astype(F32)
            first = (part * HALVES + half) * LANE
            for copy in range(copies_ref.shape[0]):
                copies_ref[copy, :, first : first + LANE] = total.astype(BF16)


def frame_kernel(
    arrived_ref, toks_ref, kernel_far, back_ref, ahead_ref, out_ref,
    shifted, taps, low, high, kernel_here, sem, spread,
):
    frame_count = out_ref.shape[0]
    rows = shifted.shape[1]
    columns = 2 * arrived_ref.shape[0]
    spread[...] = arrived_ref[:, :EDGE, :].astype(F32).reshape(columns * ROWS, LANE)
    chosen = down_rows(toks_ref[...] & columns - 1, rows)
    onehot = chosen == lax.broadcasted_iota(I32, (rows, columns), 1).astype(F32)
    onehot = jnp.where(onehot, 1.0, 0.0).astype(BF16)
    for part in range(ROWS):
        shifted[0, :, part * LANE : (part + 1) * LANE] = jnp.dot(
            onehot,
            spread[pl.ds(part, columns, stride=ROWS), :].astype(BF16),
            preferred_element_type=F32,
        )
    low[...] = down_rows(back_ref[...], frame_count)
    high[...] = down_rows(ahead_ref[...], frame_count)
    prepare(shifted, taps, kernel_far, kernel_here, sem)
    convolve(shifted, taps, low, high, 1, EDGE, out_ref, frame_count // EDGE)


SMALL, LARGE = pl.BlockSpec(memory_space=pltpu.SMEM), pl.BlockSpec(memory_space=pltpu.VMEM)
FAR = pl.BlockSpec(memory_space=pltpu.HBM)


def far(array):
    return pltpu.with_memory_space_constraint(array, pltpu.HBM)


def call(kernel, outs, scratch, flops, moved, ins=None, mib=16):
    options = {} if ins is None else {"in_specs": ins}
    return pl.pallas_call(
        kernel,
        out_shape=outs,
        scratch_shapes=scratch,
        compiler_params=pltpu.CompilerParams(vmem_limit_bytes=mib * 1024 * 1024),
        cost_estimate=pl.CostEstimate(flops=flops, bytes_accessed=moved, transcendentals=0),
        **options,
    )


def all_to_all(blocks, axis):
    return lax.all_to_all(blocks, axis, split_axis=0, concat_axis=0, tiled=True)


def body(tokens, text_weight, conv_kernel, frame_token, seg_before, seg_after, cotangent):
    peers = lax.axis_size("seq")
    shards = lax.axis_size("dp")
    rank = lax.axis_index("seq")
    slots, block_rows, width = tokens.shape[1], tokens.shape[3], tokens.shape[4]
    half_span = conv_kernel.shape[0] // 2
    frame_count = cotangent.shape[1]
    own_rows = slots * block_rows
    cot = cotangent[0]
    rank_word = rank[None]

    rim = jax.ShapeDtypeStruct((LEAD, width), BF16)
    line = jax.ShapeDtypeStruct((1, frame_count), I32)
    blocks = tokens.reshape(slots, block_rows, width)
    given = [far(array) for array in (cot, frame_token, seg_before, seg_after, blocks)]
    tail, cot, toks, back, ahead, normed = call(
        rim_kernel,
        [rim, jax.ShapeDtypeStruct(cot.shape, BF16), line, line, line]
        + [jax.ShapeDtypeStruct((own_rows, width), BF16)],
        [
            pltpu.VMEM((ROWS, width), F32),
            pltpu.VMEM(blocks.shape, BF16),
            pltpu.SemaphoreType.DMA((len(given),)),
        ],
        8 * EDGE * width,
        4 * frame_count * width,
        [FAR] * len(given),
        mib=4,
    )(*given)
    before = lax.ppermute(tail, "seq", [(i, i + 1) for i in range(peers - 1)])
    text_rows = call(
        text_kernel,
        jax.ShapeDtypeStruct((own_rows, width), BF16),
        [],
        2 * own_rows * width * width,
        24 * width * width,
        mib=8,
    )(normed, text_weight)

    def hop(count):
        path = [(i, i // MEMBERS * MEMBERS + (i + 2 * count) % MEMBERS) for i in range(peers)]
        return lax.ppermute(normed, "seq", path)

    pieces = [normed] + [hop(count) for count in range(1, MEMBERS // 2)]

    def scratch(rows, frames):
        return [
            pltpu.VMEM((ROWS, rows, width), F32),
            pltpu.VMEM((conv_kernel.shape[0], ROWS, width), F32),
            pltpu.VMEM((frames, LANE), F32),
            pltpu.VMEM((frames, LANE), F32),
            pltpu.VMEM(conv_kernel.shape, BF16),
            pltpu.SemaphoreType.DMA,
        ]

    work = 12 * conv_kernel.shape[0] * frame_count * width
    packed = call(
        grad_kernel,
        jax.ShapeDtypeStruct((peers, EDGE + ROWS, LANE), BF16),
        scratch(LEAD + frame_count + EDGE, frame_count + EDGE)
        + [pltpu.VMEM((frame_count + EDGE, width), BF16)],
        work,
        4 * frame_count * width,
        [SMALL] + [LARGE] * 2 + [FAR] + [LARGE] * 3,
    )(rank_word, cot, before, far(conv_kernel), back, ahead, toks)
    returned = all_to_all(packed, "seq")
    same, text_rows = lax.optimization_barrier((jnp.concatenate(pieces), text_rows))
    other = lax.ppermute(same, "seq", [(i, i ^ 1) for i in range(peers)])

    def joined(upper, lower):
        return (upper.astype(I32) << SPLIT_BITS) + lower.astype(I32)

    ends = slice(frame_count - half_span, frame_count)
    none = jnp.zeros((1,), I32)
    ahead_notes = lax.dynamic_index_in_dim(
        returned[:, EDGE : EDGE + ROWS, :half_span], (rank + 1) % peers, keepdims=False
    )
    all_toks = jnp.concatenate(
        [
            none,
            joined(before[0, ends], before[0, LOW_AT:][ends]),
            toks[0],
            joined(ahead_notes[4], ahead_notes[6]),
            none,
        ]
    )[None]
    product = call(
        lambda *refs: product_kernel(
            *refs, slots=slots, block_rows=block_rows, frame_count=frame_count
        ),
        jax.ShapeDtypeStruct((peers, EDGE * (1 + HALVES), LANE), BF16),
        [
            pltpu.VMEM((peers * ROWS, LANE), F32),
            pltpu.VMEM((MEMBERS // 2 * own_rows, width), BF16),
            pltpu.VMEM((peers * EDGE, LANE), F32),
            pltpu.SemaphoreType.DMA,
        ],
        4 * MEMBERS * own_rows * width * LANE * HALVES,
        4 * MEMBERS * own_rows * width,
        [SMALL] + [LARGE] * 2 + [FAR, LARGE],
        24,
    )(rank_word, returned, text_rows, far(same), other)
    arrived = all_to_all(product, "seq")

    copies = call(
        share_kernel,
        jax.ShapeDtypeStruct((shards, width // peers, width), BF16),
        [],
        peers * EDGE * HALVES * LANE,
        peers * EDGE * HALVES * LANE,
    )(arrived)
    shares = all_to_all(copies, "dp")
    summed = jnp.sum(shares.astype(F32), axis=0)

    frames_out = call(
        frame_kernel,
        jax.ShapeDtypeStruct((frame_count, width), BF16),
        scratch(frame_count + 2 * EDGE, frame_count) + [pltpu.VMEM((peers * EDGE, LANE), F32)],
        work,
        4 * frame_count * width,
        [LARGE] * 2 + [FAR] + [LARGE] * 2,
    )(arrived, all_toks, far(conv_kernel), back, ahead)
    return (frames_out[None], summed)


def solution(mesh):
    in_specs = (
        P("dp", None, "seq", None, None),
        P(),
        P(),
        P("dp", "seq"),
        P("dp", "seq"),
        P("dp", "seq"),
        P("dp", "seq", None),
    )
    out_specs = (P("dp", "seq", None), P("seq", None))
    return jax.shard_map(body, mesh=mesh, in_specs=in_specs, out_specs=out_specs, check_vma=False)
```

```python
import jax
import jax.numpy as jnp
from jax import lax
from jax.experimental import pallas as pl
from jax.experimental.pallas import tpu as pltpu
from jax.sharding import PartitionSpec as P

EDGE = 16
LEAD = 32
SPLIT_BITS = 6
LOW_AT, BACK_AT, AHEAD_AT = 256, 512, 768
ROWS = 8
LANE = 128
FOLD = 4
MEMBERS = 8
HALVES = ROWS // MEMBERS
F32, BF16, I32 = jnp.float32, jnp.bfloat16, jnp.int32


def rms_rows(rows):
    wide = rows.astype(F32)
    scale = lax.rsqrt(jnp.mean(wide * wide, axis=-1, keepdims=True) + 1e-06)
    return (wide * scale).astype(BF16)


def rim_kernel(
    cot_any, toks_any, back_any, ahead_any, own_any,
    tail_ref, cot_ref, toks_ref, back_ref, ahead_ref, normed_ref, note, own, sems,
):
    pairs = (
        (cot_any, cot_ref), (toks_any, toks_ref), (back_any, back_ref), (ahead_any, ahead_ref),
        (own_any, own),
    )
    moves = [
        pltpu.make_async_copy(source, target, sems.at[index])
        for index, (source, target) in enumerate(pairs)
    ]
    for move in moves:
        move.start()
    note[...] = jnp.zeros_like(note)
    for move in moves:
        move.wait()
    frame_count = toks_ref.shape[1]
    toks = toks_ref[...]
    values = (toks >> SPLIT_BITS, toks & (1 << SPLIT_BITS) - 1, back_ref[...], ahead_ref[...])
    for at, value in zip((0, LOW_AT, BACK_AT, AHEAD_AT), values):
        note[:1, at : at + frame_count] = value.astype(F32)
    line = lax.broadcasted_iota(I32, tail_ref.shape, 0)
    last = cot_ref[frame_count - LEAD :].astype(F32)
    tail_ref[...] = jnp.where(line == 0, note[:1], last).astype(BF16)
    normed_ref[...] = rms_rows(own[...].astype(F32).reshape(normed_ref.shape))


def text_kernel(normed_ref, weight_ref, text_ref):
    text_ref[...] = jnp.dot(
        normed_ref[...], weight_ref[...], preferred_element_type=F32
    ).astype(BF16)


def down_rows(row, count):
    square = (count, count)
    here = lax.broadcasted_iota(jnp.int32, square, 0) == lax.broadcasted_iota(jnp.int32, square, 1)
    diagonal = jnp.where(here, row.astype(F32), 0.0).astype(BF16)
    return jnp.dot(diagonal, jnp.ones((count, LANE), BF16), preferred_element_type=F32)


def prepare(shifted, taps, kernel_far, kernel_here, sem):
    move = pltpu.make_async_copy(kernel_far, kernel_here, sem)
    move.start()
    rows, width = shifted.shape[1], shifted.shape[2]

    def shift(block, _):
        lanes = pl.ds(pl.multiple_of(block * LANE, LANE), LANE)
        window = shifted[0, :, lanes]
        for by in range(1, ROWS):
            shifted[by, :, lanes] = pltpu.roll(window, rows - by, 0)
        return 0

    lax.fori_loop(0, width // LANE, shift, 0)
    move.wait()
    wide = kernel_here[...].astype(F32)
    for tap in range(wide.shape[0]):
        taps[tap] = jnp.broadcast_to(wide[tap : tap + 1], (ROWS, width))


def convolve(shifted, taps, low, high, direction, first_row, out_ref, chunks):
    half_span = taps.shape[0] // 2
    blocks = shifted.shape[2] // LANE
    step = 2 * ROWS

    def chunk(index, _):
        base = pl.multiple_of(index * step, step)
        totals = [[None] * blocks for _ in range(2)]
        lows = [low[pl.ds(base + part * ROWS, ROWS), :] for part in range(2)]
        highs = [high[pl.ds(base + part * ROWS, ROWS), :] for part in range(2)]
        order = [0] + [k for far in range(1, half_span + 1) for k in (-far, far)]
        for shift_by in order:
            row = first_row + direction * shift_by
            by, first = row % ROWS, row // ROWS * ROWS
            if shift_by < 0:
                inside = [value >= float(-shift_by) for value in lows]
            else:
                inside = [value >= float(shift_by) for value in highs]
            for block in range(blocks):
                lanes = slice(block * LANE, (block + 1) * LANE)
                tap = taps[shift_by + half_span, :, lanes]
                for part in range(2):
                    values = shifted[by, pl.ds(base + first + part * ROWS, ROWS), lanes]
                    term = tap * values
                    if shift_by == 0:
                        totals[part][block] = values + term
                    else:
                        totals[part][block] += jnp.where(inside[part], term, 0.0)
        for block in range(blocks):
            lanes = slice(block * LANE, (block + 1) * LANE)
            both = jnp.concatenate([totals[0][block], totals[1][block]], axis=0)
            out_ref[pl.ds(base, step), lanes] = both.astype(BF16)
        return 0

    lax.fori_loop(0, chunks, chunk, 0)


def grad_kernel(
    rank_ref, cot_ref, before_ref, kernel_far, back_ref, ahead_ref, toks_ref, out_ref,
    shifted, taps, low, high, kernel_here, sem, frame_grad,
):
    frame_count, width = cot_ref.shape
    peers = out_ref.shape[0]
    columns = 2 * peers
    last = jnp.where(rank_ref[0] == peers - 1, 1, 0)
    shifted[0, :LEAD, :] = before_ref[...].astype(F32)
    shifted[0, LEAD : LEAD + frame_count, :] = cot_ref[...].astype(F32)
    shifted[0, LEAD + frame_count :, :] = jnp.zeros((EDGE, width), F32)
    count, half_span = frame_grad.shape[0], taps.shape[0] // 2
    shape = (count, frame_count)
    line, lane = lax.broadcasted_iota(I32, shape, 0), lax.broadcasted_iota(I32, shape, 1)
    ours, theirs = lane == line - half_span, lane == line - half_span + frame_count
    note = before_ref[:EDGE, :].astype(F32)[:1]

    def of_frames(their, own):
        chosen = jnp.where(ours, own.astype(F32), jnp.where(theirs, their, 0.0)).astype(BF16)
        ones = jnp.ones((frame_count, LANE), BF16)
        return jnp.dot(chosen, ones, preferred_element_type=F32)

    low[...] = of_frames(note[:, AHEAD_AT : AHEAD_AT + frame_count], ahead_ref[...])
    high[...] = of_frames(note[:, BACK_AT : BACK_AT + frame_count], back_ref[...])
    prepare(shifted, taps, kernel_far, kernel_here, sem)
    frame_grad[frame_count:] = jnp.zeros((EDGE, width), BF16)
    first_row = LEAD - half_span
    convolve(
        shifted, taps, low, high, -1, first_row, frame_grad, frame_count // EDGE + last
    )
    their = note[:, :frame_count] * float(1 << SPLIT_BITS) + note[:, LOW_AT : LOW_AT + frame_count]
    their = (their.astype(I32) & columns - 1).astype(F32)
    chosen = of_frames(their, toks_ref[...] & columns - 1)
    place = lax.broadcasted_iota(I32, chosen.shape, 0)
    end = frame_count + last * half_span
    spot = lax.broadcasted_iota(I32, chosen.shape, 1).astype(F32)
    onehot = jnp.where((chosen == spot) & (place < end), 1.0, 0.0).astype(BF16)
    sums = lax.dot_general(
        onehot, frame_grad[...], (((0,), (0,)), ((), ())), preferred_element_type=F32
    )
    at = note_at(frame_count) // LANE * LANE
    line = lax.broadcasted_iota(I32, (ROWS, LANE), 0)
    own = toks_ref[:, :LANE]
    lines = (
        note[:, at : at + LANE],
        note[:, LOW_AT + at : LOW_AT + at + LANE],
        (own >> SPLIT_BITS).astype(F32),
        (own & (1 << SPLIT_BITS) - 1).astype(F32),
    )
    marks = jnp.zeros((ROWS, LANE), F32)
    for index, value in enumerate(lines):
        marks = jnp.where(line == index, value, marks)
    marks = marks[:FOLD].astype(BF16)
    for peer in range(peers):
        group, part = peer // MEMBERS, peer % MEMBERS
        rows = slice(group * 2 * MEMBERS, (group + 1) * 2 * MEMBERS)
        first = part * HALVES * LANE
        block = [
            sums[rows, first + half * LANE : first + (half + 1) * LANE] for half in range(HALVES)
        ]
        block = jnp.concatenate(block, axis=0)
        for piece in range(FOLD):
            out_ref[peer, :, piece * LANE : (piece + 1) * LANE] = block[
                piece * FOLD : (piece + 1) * FOLD
            ].astype(BF16)
        out_ref[peer, :, FOLD * LANE :] = marks


def note_at(frame_count):
    return frame_count - EDGE + 1


def product_kernel(
    rank_ref, returned_ref, text_ref, same_far, other_ref, out_ref, marks, normed, spread, sems,
    *, slots, block_rows, frame_count,
):
    peers = returned_ref.shape[0]
    rows, width = text_ref.shape
    terms = peers * EDGE
    rank = rank_ref[0]
    share = same_far.shape[0] // sems.shape[0]
    moves = [
        pltpu.make_async_copy(
            same_far.at[pl.ds(index * share, share)],
            normed.at[pl.ds(index * share, share)],
            sems.at[index],
        )
        for index in range(sems.shape[0])
    ]
    for move in moves:
        move.start()

    note = returned_ref[:, :, FOLD * LANE :].astype(F32).reshape(peers * FOLD, LANE)
    line = lax.broadcasted_iota(I32, (LANE, LANE), 0)
    chosen = jnp.where(line == note_at(frame_count) % LANE, 1.0, 0.0).astype(BF16)
    marks[...] = jnp.dot(note.astype(BF16), chosen, preferred_element_type=F32)
    upper = marks[pl.ds(0, peers, stride=FOLD), :]
    lower = marks[pl.ds(1, peers, stride=FOLD), :]
    shape = (peers, terms)
    term = lax.broadcasted_iota(I32, shape, 1)
    here = (term & FOLD * peers - 1) // FOLD == lax.broadcasted_iota(I32, shape, 0)

    def along(values):
        wide = jnp.concatenate([values] * (terms // LANE), axis=1)
        wide = jnp.where(here, wide, 0.0).astype(BF16)
        ones = jnp.ones((ROWS, peers), BF16)
        return jnp.dot(ones, wide, preferred_element_type=F32)[:1]

    def block_of(upper, lower):
        return ((upper.astype(I32) << SPLIT_BITS) + lower.astype(I32)) // block_rows

    def slot_of(starts, lane):
        return (starts + (lane - starts & peers - 1)) // peers

    starts = block_of(along(upper), along(lower))
    term = lax.broadcasted_iota(I32, (1, terms), 1)
    term = term // (FOLD * peers) * FOLD + (term & FOLD - 1)
    member = term // block_rows & MEMBERS - 1
    half = term // (block_rows * MEMBERS) & HALVES - 1
    slot = slot_of(starts, rank // MEMBERS * MEMBERS + member)
    total = MEMBERS * rows
    chips = MEMBERS // 2
    away = ((rank & MEMBERS - 1) // 2 - member // 2) & chips - 1
    target = half * total + ((rank ^ member) & 1) * chips * rows + away * rows
    target = target + slot * block_rows + (term & block_rows - 1)
    target = jnp.where(slot < slots, target, -1)
    onehot = lax.broadcasted_iota(I32, (HALVES * total, terms), 0) == target
    sums = jnp.concatenate(
        [
            returned_ref[:, :, piece * LANE : (piece + 1) * LANE]
            .astype(F32)
            .reshape(peers * FOLD, LANE)
            for piece in range(FOLD)
        ],
        axis=0,
    ).astype(BF16)
    token_grad = jnp.dot(
        jnp.where(onehot, 1.0, 0.0).astype(BF16),
        sums,
        preferred_element_type=F32,
    )
    mine = slot_of(block_of(upper, lower), rank)[:, :rows]
    mine = jnp.minimum(mine, slots - 1) * block_rows
    column = lax.broadcasted_iota(I32, (peers, rows), 1)
    for row in range(block_rows):
        picks = jnp.where(column == mine + row, 1.0, 0.0).astype(BF16)
        picked = jnp.dot(picks, text_ref[...], preferred_element_type=F32)
        for part in range(ROWS):
            spread[pl.ds(row * ROWS + part, peers, stride=EDGE), :] = picked[
                :, part * LANE : (part + 1) * LANE
            ]
    out_ref[:, :EDGE, :] = spread[...].astype(BF16).reshape(peers, EDGE, LANE)

    for move in moves:
        move.wait()
    for part in range(HALVES):
        grad = token_grad[part * total : (part + 1) * total]
        first = grad.astype(BF16)
        second = (grad - first.astype(F32)).astype(BF16)
        both = jnp.concatenate([first, second], axis=1)
        product = jnp.zeros((width, 2 * LANE), F32)
        for index, ref in enumerate((normed, other_ref)):
            rows_of = slice(index * total // 2, (index + 1) * total // 2)
            product += lax.dot_general(
                ref[...], both[rows_of], (((0,), (0,)), ((), ())), preferred_element_type=F32
            )
        product = (product[:, :LANE] + product[:, LANE:]).astype(BF16)
        out_ref[:, EDGE * (part + 1) : EDGE * (part + 2), :] = product.reshape(peers, EDGE, LANE)


def share_kernel(arrived_ref, copies_ref):
    peers = arrived_ref.shape[0]
    for part in range(MEMBERS):
        for half in range(HALVES):
            total = jnp.zeros((EDGE, LANE), F32)
            for group in range(peers // MEMBERS):
                total += arrived_ref[
                    group * MEMBERS + part, EDGE * (half + 1) : EDGE * (half + 2), :
                ].astype(F32)
            first = (part * HALVES + half) * LANE
            for copy in range(copies_ref.shape[0]):
                copies_ref[copy, :, first : first + LANE] = total.astype(BF16)


def frame_kernel(
    arrived_ref, toks_ref, kernel_far, back_ref, ahead_ref, out_ref,
    shifted, taps, low, high, kernel_here, sem, spread,
):
    frame_count = out_ref.shape[0]
    rows = shifted.shape[1]
    columns = 2 * arrived_ref.shape[0]
    spread[...] = arrived_ref[:, :EDGE, :].astype(F32).reshape(columns * ROWS, LANE)
    chosen = down_rows(toks_ref[...] & columns - 1, rows)
    onehot = chosen == lax.broadcasted_iota(I32, (rows, columns), 1).astype(F32)
    onehot = jnp.where(onehot, 1.0, 0.0).astype(BF16)
    for part in range(ROWS):
        shifted[0, :, part * LANE : (part + 1) * LANE] = jnp.dot(
            onehot,
            spread[pl.ds(part, columns, stride=ROWS), :].astype(BF16),
            preferred_element_type=F32,
        )
    low[...] = down_rows(back_ref[...], frame_count)
    high[...] = down_rows(ahead_ref[...], frame_count)
    prepare(shifted, taps, kernel_far, kernel_here, sem)
    convolve(shifted, taps, low, high, 1, EDGE, out_ref, frame_count // EDGE)


SMALL, LARGE = pl.BlockSpec(memory_space=pltpu.SMEM), pl.BlockSpec(memory_space=pltpu.VMEM)
FAR = pl.BlockSpec(memory_space=pltpu.HBM)


def far(array):
    return pltpu.with_memory_space_constraint(array, pltpu.HBM)


def call(kernel, outs, scratch, flops, moved, ins=None, mib=16):
    options = {} if ins is None else {"in_specs": ins}
    return pl.pallas_call(
        kernel,
        out_shape=outs,
        scratch_shapes=scratch,
        compiler_params=pltpu.CompilerParams(vmem_limit_bytes=mib * 1024 * 1024),
        cost_estimate=pl.CostEstimate(flops=flops, bytes_accessed=moved, transcendentals=0),
        **options,
    )


def all_to_all(blocks, axis):
    return lax.all_to_all(blocks, axis, split_axis=0, concat_axis=0, tiled=True)


def body(tokens, text_weight, conv_kernel, frame_token, seg_before, seg_after, cotangent):
    peers = lax.axis_size("seq")
    shards = lax.axis_size("dp")
    rank = lax.axis_index("seq")
    slots, block_rows, width = tokens.shape[1], tokens.shape[3], tokens.shape[4]
    half_span = conv_kernel.shape[0] // 2
    frame_count = cotangent.shape[1]
    own_rows = slots * block_rows
    cot = cotangent[0]
    rank_word = rank[None]

    rim = jax.ShapeDtypeStruct((LEAD, width), BF16)
    line = jax.ShapeDtypeStruct((1, frame_count), I32)
    blocks = tokens.reshape(slots, block_rows, width)
    given = [far(array) for array in (cot, frame_token, seg_before, seg_after, blocks)]
    tail, cot, toks, back, ahead, normed = call(
        rim_kernel,
        [rim, jax.ShapeDtypeStruct(cot.shape, BF16), line, line, line]
        + [jax.ShapeDtypeStruct((own_rows, width), BF16)],
        [
            pltpu.VMEM((ROWS, width), F32),
            pltpu.VMEM(blocks.shape, BF16),
            pltpu.SemaphoreType.DMA((len(given),)),
        ],
        8 * EDGE * width,
        4 * frame_count * width,
        [FAR] * len(given),
        mib=4,
    )(*given)
    before = lax.ppermute(tail, "seq", [(i, i + 1) for i in range(peers - 1)])
    def hop(rows, count):
        path = [(i, i // MEMBERS * MEMBERS + (i + 2 * count) % MEMBERS) for i in range(peers)]
        return lax.ppermute(rows, "seq", path)

    near = [hop(normed, 1), hop(normed, 3)]

    def scratch(rows, frames):
        return [
            pltpu.VMEM((ROWS, rows, width), F32),
            pltpu.VMEM((conv_kernel.shape[0], ROWS, width), F32),
            pltpu.VMEM((frames, LANE), F32),
            pltpu.VMEM((frames, LANE), F32),
            pltpu.VMEM(conv_kernel.shape, BF16),
            pltpu.SemaphoreType.DMA,
        ]

    work = 12 * conv_kernel.shape[0] * frame_count * width
    packed = call(
        grad_kernel,
        jax.ShapeDtypeStruct((peers, FOLD, (FOLD + 1) * LANE), BF16),
        scratch(LEAD + frame_count + EDGE, frame_count + EDGE)
        + [pltpu.VMEM((frame_count + EDGE, width), BF16)],
        work,
        4 * frame_count * width,
        [SMALL] + [LARGE] * 2 + [FAR] + [LARGE] * 3,
    )(rank_word, cot, before, far(conv_kernel), back, ahead, toks)
    later, packed = lax.optimization_barrier((normed, packed))
    text_rows = call(
        text_kernel,
        jax.ShapeDtypeStruct((own_rows, width), BF16),
        [],
        2 * own_rows * width * width,
        24 * width * width,
        mib=8,
    )(later, text_weight)
    pieces = [normed, near[0], hop(later, 2), near[1]]
    same, text_rows = lax.optimization_barrier((jnp.concatenate(pieces), text_rows))
    other = lax.ppermute(same, "seq", [(i, i ^ 1) for i in range(peers)])

    returned = all_to_all(packed, "seq")

    def joined(upper, lower):
        return (upper.astype(I32) << SPLIT_BITS) + lower.astype(I32)

    ends = slice(frame_count - half_span, frame_count)
    none = jnp.zeros((1,), I32)
    ahead_notes = lax.dynamic_index_in_dim(
        returned[:, :, FOLD * LANE : FOLD * LANE + half_span], (rank + 1) % peers, keepdims=False
    )
    all_toks = jnp.concatenate(
        [
            none,
            joined(before[0, ends], before[0, LOW_AT:][ends]),
            toks[0],
            joined(ahead_notes[2], ahead_notes[3]),
            none,
        ]
    )[None]
    product = call(
        lambda *refs: product_kernel(
            *refs, slots=slots, block_rows=block_rows, frame_count=frame_count
        ),
        jax.ShapeDtypeStruct((peers, EDGE * (1 + HALVES), LANE), BF16),
        [
            pltpu.VMEM((peers * FOLD, LANE), F32),
            pltpu.VMEM((MEMBERS // 2 * own_rows, width), BF16),
            pltpu.VMEM((peers * EDGE, LANE), F32),
            pltpu.SemaphoreType.DMA((4,)),
        ],
        4 * MEMBERS * own_rows * width * LANE * HALVES,
        4 * MEMBERS * own_rows * width,
        [SMALL] + [LARGE] * 2 + [FAR, LARGE],
        24,
    )(rank_word, returned, text_rows, far(same), other)
    arrived = all_to_all(product, "seq")

    copies = call(
        share_kernel,
        jax.ShapeDtypeStruct((shards, width // peers, width), BF16),
        [],
        peers * EDGE * HALVES * LANE,
        peers * EDGE * HALVES * LANE,
    )(arrived)
    shares = all_to_all(copies, "dp")
    summed = jnp.sum(shares.astype(F32), axis=0)

    frames_out = call(
        frame_kernel,
        jax.ShapeDtypeStruct((frame_count, width), BF16),
        scratch(frame_count + 2 * EDGE, frame_count) + [pltpu.VMEM((peers * EDGE, LANE), F32)],
        work,
        4 * frame_count * width,
        [LARGE] * 2 + [FAR] + [LARGE] * 2,
    )(arrived, all_toks, far(conv_kernel), back, ahead)
    return (frames_out[None], summed)


def solution(mesh):
    in_specs = (
        P("dp", None, "seq", None, None),
        P(),
        P(),
        P("dp", "seq"),
        P("dp", "seq"),
        P("dp", "seq"),
        P("dp", "seq", None),
    )
    out_specs = (P("dp", "seq", None), P("seq", None))
    return jax.shard_map(body, mesh=mesh, in_specs=in_specs, out_specs=out_specs, check_vma=False)
```

```python
import jax
import jax.numpy as jnp
from jax import lax
from jax.experimental import pallas as pl
from jax.experimental.pallas import tpu as pltpu
from jax.sharding import PartitionSpec as P

EDGE = 16
LEAD = 32
SPLIT_BITS = 6
LOW_AT, BACK_AT, AHEAD_AT = 256, 512, 768
ROWS = 8
LANE = 128
FOLD = 4
MEMBERS = 8
HALVES = ROWS // MEMBERS
F32, BF16, I32 = jnp.float32, jnp.bfloat16, jnp.int32


def rms_rows(rows):
    wide = rows.astype(F32)
    scale = lax.rsqrt(jnp.mean(wide * wide, axis=-1, keepdims=True) + 1e-06)
    return (wide * scale).astype(BF16)


def rim_kernel(
    cot_any, toks_any, back_any, ahead_any, own_any,
    tail_ref, cot_ref, toks_ref, back_ref, ahead_ref, normed_ref, note, own, sems,
):
    pairs = (
        (cot_any, cot_ref), (toks_any, toks_ref), (back_any, back_ref), (ahead_any, ahead_ref),
        (own_any, own),
    )
    moves = [
        pltpu.make_async_copy(source, target, sems.at[index])
        for index, (source, target) in enumerate(pairs)
    ]
    for move in moves:
        move.start()
    note[...] = jnp.zeros_like(note)
    for move in moves:
        move.wait()
    frame_count = toks_ref.shape[1]
    toks = toks_ref[...]
    values = (toks >> SPLIT_BITS, toks & (1 << SPLIT_BITS) - 1, back_ref[...], ahead_ref[...])
    for at, value in zip((0, LOW_AT, BACK_AT, AHEAD_AT), values):
        note[:1, at : at + frame_count] = value.astype(F32)
    line = lax.broadcasted_iota(I32, tail_ref.shape, 0)
    last = cot_ref[frame_count - LEAD :].astype(F32)
    tail_ref[...] = jnp.where(line == 0, note[:1], last).astype(BF16)
    normed_ref[...] = rms_rows(own[...].astype(F32).reshape(normed_ref.shape))


def text_kernel(normed_ref, weight_ref, text_ref):
    text_ref[...] = jnp.dot(
        normed_ref[...], weight_ref[...], preferred_element_type=F32
    ).astype(BF16)


def down_rows(row, count):
    square = (count, count)
    here = lax.broadcasted_iota(jnp.int32, square, 0) == lax.broadcasted_iota(jnp.int32, square, 1)
    diagonal = jnp.where(here, row.astype(F32), 0.0).astype(BF16)
    return jnp.dot(diagonal, jnp.ones((count, LANE), BF16), preferred_element_type=F32)


def prepare(shifted, taps, kernel_far, kernel_here, sem):
    move = pltpu.make_async_copy(kernel_far, kernel_here, sem)
    move.start()
    rows, width = shifted.shape[1], shifted.shape[2]

    def shift(block, _):
        lanes = pl.ds(pl.multiple_of(block * LANE, LANE), LANE)
        window = shifted[0, :, lanes]
        for by in range(1, ROWS):
            shifted[by, :, lanes] = pltpu.roll(window, rows - by, 0)
        return 0

    lax.fori_loop(0, width // LANE, shift, 0)
    move.wait()
    wide = kernel_here[...].astype(F32)
    for tap in range(wide.shape[0]):
        taps[tap] = jnp.broadcast_to(wide[tap : tap + 1], (ROWS, width))


def convolve(shifted, taps, low, high, direction, first_row, out_ref, chunks):
    half_span = taps.shape[0] // 2
    blocks = shifted.shape[2] // LANE
    step = 2 * ROWS

    def chunk(index, _):
        base = pl.multiple_of(index * step, step)
        totals = [[None] * blocks for _ in range(2)]
        lows = [low[pl.ds(base + part * ROWS, ROWS), :] for part in range(2)]
        highs = [high[pl.ds(base + part * ROWS, ROWS), :] for part in range(2)]
        order = [0] + [k for far in range(1, half_span + 1) for k in (-far, far)]
        for shift_by in order:
            row = first_row + direction * shift_by
            by, first = row % ROWS, row // ROWS * ROWS
            if shift_by < 0:
                inside = [value >= float(-shift_by) for value in lows]
            else:
                inside = [value >= float(shift_by) for value in highs]
            for block in range(blocks):
                lanes = slice(block * LANE, (block + 1) * LANE)
                tap = taps[shift_by + half_span, :, lanes]
                for part in range(2):
                    values = shifted[by, pl.ds(base + first + part * ROWS, ROWS), lanes]
                    term = tap * values
                    if shift_by == 0:
                        totals[part][block] = values + term
                    else:
                        totals[part][block] += jnp.where(inside[part], term, 0.0)
        for block in range(blocks):
            lanes = slice(block * LANE, (block + 1) * LANE)
            both = jnp.concatenate([totals[0][block], totals[1][block]], axis=0)
            out_ref[pl.ds(base, step), lanes] = both.astype(BF16)
        return 0

    lax.fori_loop(0, chunks, chunk, 0)


def grad_kernel(
    rank_ref, cot_ref, before_ref, kernel_far, back_ref, ahead_ref, toks_ref, out_ref,
    shifted, taps, low, high, kernel_here, sem, frame_grad,
):
    frame_count, width = cot_ref.shape
    peers = out_ref.shape[0]
    columns = 2 * peers
    last = jnp.where(rank_ref[0] == peers - 1, 1, 0)
    shifted[0, :LEAD, :] = before_ref[...].astype(F32)
    shifted[0, LEAD : LEAD + frame_count, :] = cot_ref[...].astype(F32)
    shifted[0, LEAD + frame_count :, :] = jnp.zeros((EDGE, width), F32)
    count, half_span = frame_grad.shape[0], taps.shape[0] // 2
    shape = (count, frame_count)
    line, lane = lax.broadcasted_iota(I32, shape, 0), lax.broadcasted_iota(I32, shape, 1)
    ours, theirs = lane == line - half_span, lane == line - half_span + frame_count
    note = before_ref[:EDGE, :].astype(F32)[:1]

    def of_frames(their, own):
        chosen = jnp.where(ours, own.astype(F32), jnp.where(theirs, their, 0.0)).astype(BF16)
        ones = jnp.ones((frame_count, LANE), BF16)
        return jnp.dot(chosen, ones, preferred_element_type=F32)

    low[...] = of_frames(note[:, AHEAD_AT : AHEAD_AT + frame_count], ahead_ref[...])
    high[...] = of_frames(note[:, BACK_AT : BACK_AT + frame_count], back_ref[...])
    prepare(shifted, taps, kernel_far, kernel_here, sem)
    frame_grad[frame_count:] = jnp.zeros((EDGE, width), BF16)
    first_row = LEAD - half_span
    convolve(
        shifted, taps, low, high, -1, first_row, frame_grad, frame_count // EDGE + last
    )
    their = note[:, :frame_count] * float(1 << SPLIT_BITS) + note[:, LOW_AT : LOW_AT + frame_count]
    their = (their.astype(I32) & columns - 1).astype(F32)
    chosen = of_frames(their, toks_ref[...] & columns - 1)
    place = lax.broadcasted_iota(I32, chosen.shape, 0)
    end = frame_count + last * half_span
    spot = lax.broadcasted_iota(I32, chosen.shape, 1).astype(F32)
    onehot = jnp.where((chosen == spot) & (place < end), 1.0, 0.0).astype(BF16)
    sums = lax.dot_general(
        onehot, frame_grad[...], (((0,), (0,)), ((), ())), preferred_element_type=F32
    )
    at = note_at(frame_count) // LANE * LANE
    line = lax.broadcasted_iota(I32, (ROWS, LANE), 0)
    own = toks_ref[:, :LANE]
    lines = (
        note[:, at : at + LANE],
        note[:, LOW_AT + at : LOW_AT + at + LANE],
        (own >> SPLIT_BITS).astype(F32),
        (own & (1 << SPLIT_BITS) - 1).astype(F32),
    )
    marks = jnp.zeros((ROWS, LANE), F32)
    for index, value in enumerate(lines):
        marks = jnp.where(line == index, value, marks)
    marks = marks[:FOLD].astype(BF16)
    for peer in range(peers):
        group, part = peer // MEMBERS, peer % MEMBERS
        rows = slice(group * 2 * MEMBERS, (group + 1) * 2 * MEMBERS)
        first = part * HALVES * LANE
        block = [
            sums[rows, first + half * LANE : first + (half + 1) * LANE] for half in range(HALVES)
        ]
        block = jnp.concatenate(block, axis=0)
        for piece in range(FOLD):
            out_ref[peer, :, piece * LANE : (piece + 1) * LANE] = block[
                piece * FOLD : (piece + 1) * FOLD
            ].astype(BF16)
        out_ref[peer, :, FOLD * LANE :] = marks


def note_at(frame_count):
    return frame_count - EDGE + 1


def product_kernel(
    rank_ref, returned_ref, text_ref, same_far, other_ref, out_ref, marks, normed, spread, sems,
    *, slots, block_rows, frame_count,
):
    peers = returned_ref.shape[0]
    rows, width = text_ref.shape
    terms = peers * EDGE
    rank = rank_ref[0]
    share = same_far.shape[0] // sems.shape[0]
    moves = [
        pltpu.make_async_copy(
            same_far.at[pl.ds(index * share, share)],
            normed.at[pl.ds(index * share, share)],
            sems.at[index],
        )
        for index in range(sems.shape[0])
    ]
    for move in moves:
        move.start()

    note = returned_ref[:, :, FOLD * LANE :].astype(F32).reshape(peers * FOLD, LANE)
    line = lax.broadcasted_iota(I32, (LANE, LANE), 0)
    chosen = jnp.where(line == note_at(frame_count) % LANE, 1.0, 0.0).astype(BF16)
    marks[...] = jnp.dot(note.astype(BF16), chosen, preferred_element_type=F32)
    upper = marks[pl.ds(0, peers, stride=FOLD), :]
    lower = marks[pl.ds(1, peers, stride=FOLD), :]
    shape = (peers, terms)
    term = lax.broadcasted_iota(I32, shape, 1)
    here = (term & FOLD * peers - 1) // FOLD == lax.broadcasted_iota(I32, shape, 0)

    def along(values):
        wide = jnp.concatenate([values] * (terms // LANE), axis=1)
        wide = jnp.where(here, wide, 0.0).astype(BF16)
        ones = jnp.ones((ROWS, peers), BF16)
        return jnp.dot(ones, wide, preferred_element_type=F32)[:1]

    def block_of(upper, lower):
        return ((upper.astype(I32) << SPLIT_BITS) + lower.astype(I32)) // block_rows

    def slot_of(starts, lane):
        return (starts + (lane - starts & peers - 1)) // peers

    starts = block_of(along(upper), along(lower))
    term = lax.broadcasted_iota(I32, (1, terms), 1)
    term = term // (FOLD * peers) * FOLD + (term & FOLD - 1)
    member = term // block_rows & MEMBERS - 1
    half = term // (block_rows * MEMBERS) & HALVES - 1
    slot = slot_of(starts, rank // MEMBERS * MEMBERS + member)
    total = MEMBERS * rows
    chips = MEMBERS // 2
    away = ((rank & MEMBERS - 1) // 2 - member // 2) & chips - 1
    target = half * total + ((rank ^ member) & 1) * chips * rows + away * rows
    target = target + slot * block_rows + (term & block_rows - 1)
    target = jnp.where(slot < slots, target, -1)
    onehot = lax.broadcasted_iota(I32, (HALVES * total, terms), 0) == target
    sums = jnp.concatenate(
        [
            returned_ref[:, :, piece * LANE : (piece + 1) * LANE]
            .astype(F32)
            .reshape(peers * FOLD, LANE)
            for piece in range(FOLD)
        ],
        axis=0,
    ).astype(BF16)
    token_grad = jnp.dot(
        jnp.where(onehot, 1.0, 0.0).astype(BF16),
        sums,
        preferred_element_type=F32,
    )
    mine = slot_of(block_of(upper, lower), rank)[:, :rows]
    mine = jnp.minimum(mine, slots - 1) * block_rows
    column = lax.broadcasted_iota(I32, (peers, rows), 1)
    for row in range(block_rows):
        picks = jnp.where(column == mine + row, 1.0, 0.0).astype(BF16)
        picked = jnp.dot(picks, text_ref[...], preferred_element_type=F32)
        for part in range(ROWS):
            spread[pl.ds(row * ROWS + part, peers, stride=EDGE), :] = picked[
                :, part * LANE : (part + 1) * LANE
            ]
    out_ref[:, :EDGE, :] = spread[...].astype(BF16).reshape(peers, EDGE, LANE)

    for move in moves:
        move.wait()
    for part in range(HALVES):
        grad = token_grad[part * total : (part + 1) * total]
        first = grad.astype(BF16)
        second = (grad - first.astype(F32)).astype(BF16)
        both = jnp.concatenate([first, second], axis=1)
        product = jnp.zeros((width, 2 * LANE), F32)
        for index, ref in enumerate((normed, other_ref)):
            rows_of = slice(index * total // 2, (index + 1) * total // 2)
            product += lax.dot_general(
                ref[...], both[rows_of], (((0,), (0,)), ((), ())), preferred_element_type=F32
            )
        product = (product[:, :LANE] + product[:, LANE:]).astype(BF16)
        out_ref[:, EDGE * (part + 1) : EDGE * (part + 2), :] = product.reshape(peers, EDGE, LANE)


def share_kernel(arrived_ref, copies_ref):
    peers = arrived_ref.shape[0]
    for part in range(MEMBERS):
        for half in range(HALVES):
            total = jnp.zeros((EDGE, LANE), F32)
            for group in range(peers // MEMBERS):
                total += arrived_ref[
                    group * MEMBERS + part, EDGE * (half + 1) : EDGE * (half + 2), :
                ].astype(F32)
            first = (part * HALVES + half) * LANE
            for copy in range(copies_ref.shape[0]):
                copies_ref[copy, :, first : first + LANE] = total.astype(BF16)


def frame_kernel(
    arrived_ref, toks_ref, kernel_far, back_ref, ahead_ref, out_ref,
    shifted, taps, low, high, kernel_here, sem, spread,
):
    frame_count = out_ref.shape[0]
    rows = shifted.shape[1]
    columns = 2 * arrived_ref.shape[0]
    spread[...] = arrived_ref[:, :EDGE, :].astype(F32).reshape(columns * ROWS, LANE)
    chosen = down_rows(toks_ref[...] & columns - 1, rows)
    onehot = chosen == lax.broadcasted_iota(I32, (rows, columns), 1).astype(F32)
    onehot = jnp.where(onehot, 1.0, 0.0).astype(BF16)
    for part in range(ROWS):
        shifted[0, :, part * LANE : (part + 1) * LANE] = jnp.dot(
            onehot,
            spread[pl.ds(part, columns, stride=ROWS), :].astype(BF16),
            preferred_element_type=F32,
        )
    low[...] = down_rows(back_ref[...], frame_count)
    high[...] = down_rows(ahead_ref[...], frame_count)
    prepare(shifted, taps, kernel_far, kernel_here, sem)
    convolve(shifted, taps, low, high, 1, EDGE, out_ref, frame_count // EDGE)


SMALL, LARGE = pl.BlockSpec(memory_space=pltpu.SMEM), pl.BlockSpec(memory_space=pltpu.VMEM)
FAR = pl.BlockSpec(memory_space=pltpu.HBM)


def far(array):
    return pltpu.with_memory_space_constraint(array, pltpu.HBM)


def call(kernel, outs, scratch, flops, moved, ins=None, mib=16):
    options = {} if ins is None else {"in_specs": ins}
    return pl.pallas_call(
        kernel,
        out_shape=outs,
        scratch_shapes=scratch,
        compiler_params=pltpu.CompilerParams(vmem_limit_bytes=mib * 1024 * 1024),
        cost_estimate=pl.CostEstimate(flops=flops, bytes_accessed=moved, transcendentals=0),
        **options,
    )


def all_to_all(blocks, axis):
    return lax.all_to_all(blocks, axis, split_axis=0, concat_axis=0, tiled=True)


def body(tokens, text_weight, conv_kernel, frame_token, seg_before, seg_after, cotangent):
    peers = lax.axis_size("seq")
    shards = lax.axis_size("dp")
    rank = lax.axis_index("seq")
    slots, block_rows, width = tokens.shape[1], tokens.shape[3], tokens.shape[4]
    half_span = conv_kernel.shape[0] // 2
    frame_count = cotangent.shape[1]
    own_rows = slots * block_rows
    cot = cotangent[0]
    rank_word = rank[None]

    rim = jax.ShapeDtypeStruct((LEAD, width), BF16)
    line = jax.ShapeDtypeStruct((1, frame_count), I32)
    blocks = tokens.reshape(slots, block_rows, width)
    given = [far(array) for array in (cot, frame_token, seg_before, seg_after, blocks)]
    tail, cot, toks, back, ahead, normed = call(
        rim_kernel,
        [rim, jax.ShapeDtypeStruct(cot.shape, BF16), line, line, line]
        + [jax.ShapeDtypeStruct((own_rows, width), BF16)],
        [
            pltpu.VMEM((ROWS, width), F32),
            pltpu.VMEM(blocks.shape, BF16),
            pltpu.SemaphoreType.DMA((len(given),)),
        ],
        8 * EDGE * width,
        4 * frame_count * width,
        [FAR] * len(given),
        mib=4,
    )(*given)
    before = lax.ppermute(tail, "seq", [(i, i + 1) for i in range(peers - 1)])
    def hop(rows, count):
        path = [(i, i // MEMBERS * MEMBERS + (i + 2 * count) % MEMBERS) for i in range(peers)]
        return lax.ppermute(rows, "seq", path)

    near = [hop(normed, 1), hop(normed, 2)]

    def scratch(rows, frames):
        return [
            pltpu.VMEM((ROWS, rows, width), F32),
            pltpu.VMEM((conv_kernel.shape[0], ROWS, width), F32),
            pltpu.VMEM((frames, LANE), F32),
            pltpu.VMEM((frames, LANE), F32),
            pltpu.VMEM(conv_kernel.shape, BF16),
            pltpu.SemaphoreType.DMA,
        ]

    work = 12 * conv_kernel.shape[0] * frame_count * width
    packed = call(
        grad_kernel,
        jax.ShapeDtypeStruct((peers, FOLD, (FOLD + 1) * LANE), BF16),
        scratch(LEAD + frame_count + EDGE, frame_count + EDGE)
        + [pltpu.VMEM((frame_count + EDGE, width), BF16)],
        work,
        4 * frame_count * width,
        [SMALL] + [LARGE] * 2 + [FAR] + [LARGE] * 3,
    )(rank_word, cot, before, far(conv_kernel), back, ahead, toks)
    later, packed = lax.optimization_barrier((normed, packed))
    text_rows = call(
        text_kernel,
        jax.ShapeDtypeStruct((own_rows, width), BF16),
        [],
        2 * own_rows * width * width,
        24 * width * width,
        mib=8,
    )(later, text_weight)
    pieces = [normed, near[0], near[1], hop(later, 3)]
    same, text_rows = lax.optimization_barrier((jnp.concatenate(pieces), text_rows))
    other = lax.ppermute(same, "seq", [(i, i ^ 1) for i in range(peers)])

    returned = all_to_all(packed, "seq")

    def joined(upper, lower):
        return (upper.astype(I32) << SPLIT_BITS) + lower.astype(I32)

    ends = slice(frame_count - half_span, frame_count)
    none = jnp.zeros((1,), I32)
    ahead_notes = lax.dynamic_index_in_dim(
        returned[:, :, FOLD * LANE : FOLD * LANE + half_span], (rank + 1) % peers, keepdims=False
    )
    all_toks = jnp.concatenate(
        [
            none,
            joined(before[0, ends], before[0, LOW_AT:][ends]),
            toks[0],
            joined(ahead_notes[2], ahead_notes[3]),
            none,
        ]
    )[None]
    product = call(
        lambda *refs: product_kernel(
            *refs, slots=slots, block_rows=block_rows, frame_count=frame_count
        ),
        jax.ShapeDtypeStruct((peers, EDGE * (1 + HALVES), LANE), BF16),
        [
            pltpu.VMEM((peers * FOLD, LANE), F32),
            pltpu.VMEM((MEMBERS // 2 * own_rows, width), BF16),
            pltpu.VMEM((peers * EDGE, LANE), F32),
            pltpu.SemaphoreType.DMA((4,)),
        ],
        4 * MEMBERS * own_rows * width * LANE * HALVES,
        4 * MEMBERS * own_rows * width,
        [SMALL] + [LARGE] * 2 + [FAR, LARGE],
        24,
    )(rank_word, returned, text_rows, far(same), other)
    arrived = all_to_all(product, "seq")

    copies = call(
        share_kernel,
        jax.ShapeDtypeStruct((shards, width // peers, width), BF16),
        [],
        peers * EDGE * HALVES * LANE,
        peers * EDGE * HALVES * LANE,
    )(arrived)
    shares = all_to_all(copies, "dp")
    summed = jnp.sum(shares.astype(F32), axis=0)

    frames_out = call(
        frame_kernel,
        jax.ShapeDtypeStruct((frame_count, width), BF16),
        scratch(frame_count + 2 * EDGE, frame_count) + [pltpu.VMEM((peers * EDGE, LANE), F32)],
        work,
        4 * frame_count * width,
        [LARGE] * 2 + [FAR] + [LARGE] * 2,
    )(arrived, all_toks, far(conv_kernel), back, ahead)
    return (frames_out[None], summed)


def solution(mesh):
    in_specs = (
        P("dp", None, "seq", None, None),
        P(),
        P(),
        P("dp", "seq"),
        P("dp", "seq"),
        P("dp", "seq"),
        P("dp", "seq", None),
    )
    out_specs = (P("dp", "seq", None), P("seq", None))
    return jax.shard_map(body, mesh=mesh, in_specs=in_specs, out_specs=out_specs, check_vma=False)
```

```python
import jax
import jax.numpy as jnp
from jax import lax
from jax.experimental import pallas as pl
from jax.experimental.pallas import tpu as pltpu
from jax.sharding import PartitionSpec as P

EDGE = 16
LEAD = 32
SPLIT_BITS = 6
LOW_AT, BACK_AT, AHEAD_AT = 256, 512, 768
ROWS = 8
LANE = 128
FOLD = 4
MEMBERS = 8
HALVES = ROWS // MEMBERS
F32, BF16, I32 = jnp.float32, jnp.bfloat16, jnp.int32


def rms_rows(rows):
    wide = rows.astype(F32)
    scale = lax.rsqrt(jnp.mean(wide * wide, axis=-1, keepdims=True) + 1e-06)
    return (wide * scale).astype(BF16)


def rim_kernel(
    cot_any, toks_any, back_any, ahead_any, own_any,
    tail_ref, cot_ref, toks_ref, back_ref, ahead_ref, normed_ref, note, own, sems,
):
    pairs = (
        (cot_any, cot_ref), (toks_any, toks_ref), (back_any, back_ref), (ahead_any, ahead_ref),
        (own_any, own),
    )
    moves = [
        pltpu.make_async_copy(source, target, sems.at[index])
        for index, (source, target) in enumerate(pairs)
    ]
    for move in moves:
        move.start()
    note[...] = jnp.zeros_like(note)
    for move in moves:
        move.wait()
    frame_count = toks_ref.shape[1]
    toks = toks_ref[...]
    values = (toks >> SPLIT_BITS, toks & (1 << SPLIT_BITS) - 1, back_ref[...], ahead_ref[...])
    for at, value in zip((0, LOW_AT, BACK_AT, AHEAD_AT), values):
        note[:1, at : at + frame_count] = value.astype(F32)
    line = lax.broadcasted_iota(I32, tail_ref.shape, 0)
    last = cot_ref[frame_count - LEAD :].astype(F32)
    tail_ref[...] = jnp.where(line == 0, note[:1], last).astype(BF16)
    normed_ref[...] = rms_rows(own[...].astype(F32).reshape(normed_ref.shape))


def text_kernel(normed_ref, weight_ref, text_ref):
    text_ref[...] = jnp.dot(
        normed_ref[...], weight_ref[...], preferred_element_type=F32
    ).astype(BF16)


def down_rows(row, count):
    square = (count, count)
    here = lax.broadcasted_iota(jnp.int32, square, 0) == lax.broadcasted_iota(jnp.int32, square, 1)
    diagonal = jnp.where(here, row.astype(F32), 0.0).astype(BF16)
    return jnp.dot(diagonal, jnp.ones((count, LANE), BF16), preferred_element_type=F32)


def prepare(shifted, taps, kernel_far, kernel_here, sem):
    move = pltpu.make_async_copy(kernel_far, kernel_here, sem)
    move.start()
    rows, width = shifted.shape[1], shifted.shape[2]

    def shift(block, _):
        lanes = pl.ds(pl.multiple_of(block * LANE, LANE), LANE)
        window = shifted[0, :, lanes]
        for by in range(1, ROWS):
            shifted[by, :, lanes] = pltpu.roll(window, rows - by, 0)
        return 0

    lax.fori_loop(0, width // LANE, shift, 0)
    move.wait()
    wide = kernel_here[...].astype(F32)
    for tap in range(wide.shape[0]):
        taps[tap] = jnp.broadcast_to(wide[tap : tap + 1], (ROWS, width))


def convolve(shifted, taps, low, high, direction, first_row, out_ref, chunks):
    half_span = taps.shape[0] // 2
    blocks = shifted.shape[2] // LANE
    step = 2 * ROWS

    def chunk(index, _):
        base = pl.multiple_of(index * step, step)
        totals = [[None] * blocks for _ in range(2)]
        lows = [low[pl.ds(base + part * ROWS, ROWS), :] for part in range(2)]
        highs = [high[pl.ds(base + part * ROWS, ROWS), :] for part in range(2)]
        order = [0] + [k for far in range(1, half_span + 1) for k in (-far, far)]
        for shift_by in order:
            row = first_row + direction * shift_by
            by, first = row % ROWS, row // ROWS * ROWS
            if shift_by < 0:
                inside = [value >= float(-shift_by) for value in lows]
            else:
                inside = [value >= float(shift_by) for value in highs]
            for block in range(blocks):
                lanes = slice(block * LANE, (block + 1) * LANE)
                tap = taps[shift_by + half_span, :, lanes]
                for part in range(2):
                    values = shifted[by, pl.ds(base + first + part * ROWS, ROWS), lanes]
                    term = tap * values
                    if shift_by == 0:
                        totals[part][block] = values + term
                    else:
                        totals[part][block] += jnp.where(inside[part], term, 0.0)
        for block in range(blocks):
            lanes = slice(block * LANE, (block + 1) * LANE)
            both = jnp.concatenate([totals[0][block], totals[1][block]], axis=0)
            out_ref[pl.ds(base, step), lanes] = both.astype(BF16)
        return 0

    lax.fori_loop(0, chunks, chunk, 0)


def grad_kernel(
    rank_ref, cot_ref, before_ref, kernel_far, back_ref, ahead_ref, toks_ref, out_ref,
    shifted, taps, low, high, kernel_here, sem, frame_grad,
):
    frame_count, width = cot_ref.shape
    peers = out_ref.shape[0]
    columns = 2 * peers
    last = jnp.where(rank_ref[0] == peers - 1, 1, 0)
    shifted[0, :LEAD, :] = before_ref[...].astype(F32)
    shifted[0, LEAD : LEAD + frame_count, :] = cot_ref[...].astype(F32)
    shifted[0, LEAD + frame_count :, :] = jnp.zeros((EDGE, width), F32)
    count, half_span = frame_grad.shape[0], taps.shape[0] // 2
    shape = (count, frame_count)
    line, lane = lax.broadcasted_iota(I32, shape, 0), lax.broadcasted_iota(I32, shape, 1)
    ours, theirs = lane == line - half_span, lane == line - half_span + frame_count
    note = before_ref[:EDGE, :].astype(F32)[:1]

    def of_frames(their, own):
        chosen = jnp.where(ours, own.astype(F32), jnp.where(theirs, their, 0.0)).astype(BF16)
        ones = jnp.ones((frame_count, LANE), BF16)
        return jnp.dot(chosen, ones, preferred_element_type=F32)

    low[...] = of_frames(note[:, AHEAD_AT : AHEAD_AT + frame_count], ahead_ref[...])
    high[...] = of_frames(note[:, BACK_AT : BACK_AT + frame_count], back_ref[...])
    prepare(shifted, taps, kernel_far, kernel_here, sem)
    frame_grad[frame_count:] = jnp.zeros((EDGE, width), BF16)
    first_row = LEAD - half_span
    convolve(
        shifted, taps, low, high, -1, first_row, frame_grad, frame_count // EDGE + last
    )
    their = note[:, :frame_count] * float(1 << SPLIT_BITS) + note[:, LOW_AT : LOW_AT + frame_count]
    their = (their.astype(I32) & columns - 1).astype(F32)
    chosen = of_frames(their, toks_ref[...] & columns - 1)
    place = lax.broadcasted_iota(I32, chosen.shape, 0)
    end = frame_count + last * half_span
    spot = lax.broadcasted_iota(I32, chosen.shape, 1).astype(F32)
    onehot = jnp.where((chosen == spot) & (place < end), 1.0, 0.0).astype(BF16)
    sums = lax.dot_general(
        onehot, frame_grad[...], (((0,), (0,)), ((), ())), preferred_element_type=F32
    )
    at = note_at(frame_count) // LANE * LANE
    line = lax.broadcasted_iota(I32, (ROWS, LANE), 0)
    own = toks_ref[:, :LANE]
    lines = (
        note[:, at : at + LANE],
        note[:, LOW_AT + at : LOW_AT + at + LANE],
        (own >> SPLIT_BITS).astype(F32),
        (own & (1 << SPLIT_BITS) - 1).astype(F32),
    )
    marks = jnp.zeros((ROWS, LANE), F32)
    for index, value in enumerate(lines):
        marks = jnp.where(line == index, value, marks)
    marks = marks[:FOLD].astype(BF16)
    for peer in range(peers):
        group, part = peer // MEMBERS, peer % MEMBERS
        rows = slice(group * 2 * MEMBERS, (group + 1) * 2 * MEMBERS)
        first = part * HALVES * LANE
        block = [
            sums[rows, first + half * LANE : first + (half + 1) * LANE] for half in range(HALVES)
        ]
        block = jnp.concatenate(block, axis=0)
        for piece in range(FOLD):
            out_ref[peer, :, piece * LANE : (piece + 1) * LANE] = block[
                piece * FOLD : (piece + 1) * FOLD
            ].astype(BF16)
        out_ref[peer, :, FOLD * LANE :] = marks


def note_at(frame_count):
    return frame_count - EDGE + 1


def product_kernel(
    rank_ref, returned_ref, text_ref, same_far, other_ref, out_far, marks, normed, spread, sems,
    out_ref, out_sems,
    *, slots, block_rows, frame_count,
):
    peers = returned_ref.shape[0]
    rows, width = text_ref.shape
    terms = peers * EDGE
    rank = rank_ref[0]
    share = same_far.shape[0] // sems.shape[0]
    moves = [
        pltpu.make_async_copy(
            same_far.at[pl.ds(index * share, share)],
            normed.at[pl.ds(index * share, share)],
            sems.at[index],
        )
        for index in range(sems.shape[0])
    ]
    for move in moves:
        move.start()

    note = returned_ref[:, :, FOLD * LANE :].astype(F32).reshape(peers * FOLD, LANE)
    line = lax.broadcasted_iota(I32, (LANE, LANE), 0)
    chosen = jnp.where(line == note_at(frame_count) % LANE, 1.0, 0.0).astype(BF16)
    marks[...] = jnp.dot(note.astype(BF16), chosen, preferred_element_type=F32)
    upper = marks[pl.ds(0, peers, stride=FOLD), :]
    lower = marks[pl.ds(1, peers, stride=FOLD), :]
    shape = (peers, terms)
    term = lax.broadcasted_iota(I32, shape, 1)
    here = (term & FOLD * peers - 1) // FOLD == lax.broadcasted_iota(I32, shape, 0)

    def along(values):
        wide = jnp.concatenate([values] * (terms // LANE), axis=1)
        wide = jnp.where(here, wide, 0.0).astype(BF16)
        ones = jnp.ones((ROWS, peers), BF16)
        return jnp.dot(ones, wide, preferred_element_type=F32)[:1]

    def block_of(upper, lower):
        return ((upper.astype(I32) << SPLIT_BITS) + lower.astype(I32)) // block_rows

    def slot_of(starts, lane):
        return (starts + (lane - starts & peers - 1)) // peers

    starts = block_of(along(upper), along(lower))
    term = lax.broadcasted_iota(I32, (1, terms), 1)
    term = term // (FOLD * peers) * FOLD + (term & FOLD - 1)
    member = term // block_rows & MEMBERS - 1
    half = term // (block_rows * MEMBERS) & HALVES - 1
    slot = slot_of(starts, rank // MEMBERS * MEMBERS + member)
    total = MEMBERS * rows
    chips = MEMBERS // 2
    away = ((rank & MEMBERS - 1) // 2 - member // 2) & chips - 1
    target = half * total + ((rank ^ member) & 1) * chips * rows + away * rows
    target = target + slot * block_rows + (term & block_rows - 1)
    target = jnp.where(slot < slots, target, -1)
    onehot = lax.broadcasted_iota(I32, (HALVES * total, terms), 0) == target
    sums = jnp.concatenate(
        [
            returned_ref[:, :, piece * LANE : (piece + 1) * LANE]
            .astype(F32)
            .reshape(peers * FOLD, LANE)
            for piece in range(FOLD)
        ],
        axis=0,
    ).astype(BF16)
    token_grad = jnp.dot(
        jnp.where(onehot, 1.0, 0.0).astype(BF16),
        sums,
        preferred_element_type=F32,
    )
    mine = slot_of(block_of(upper, lower), rank)[:, :rows]
    mine = jnp.minimum(mine, slots - 1) * block_rows
    column = lax.broadcasted_iota(I32, (peers, rows), 1)
    for row in range(block_rows):
        picks = jnp.where(column == mine + row, 1.0, 0.0).astype(BF16)
        picked = jnp.dot(picks, text_ref[...], preferred_element_type=F32)
        for part in range(ROWS):
            spread[pl.ds(row * ROWS + part, peers, stride=EDGE), :] = picked[
                :, part * LANE : (part + 1) * LANE
            ]
    out_ref[:, :EDGE, :] = spread[...].astype(BF16).reshape(peers, EDGE, LANE)
    spans = (pl.ds(0, EDGE), pl.ds(EDGE, EDGE * HALVES))
    sends = [
        pltpu.make_async_copy(out_ref.at[:, span], out_far.at[:, span], out_sems.at[index])
        for index, span in enumerate(spans)
    ]
    sends[0].start()

    for move in moves:
        move.wait()
    for part in range(HALVES):
        grad = token_grad[part * total : (part + 1) * total]
        first = grad.astype(BF16)
        second = (grad - first.astype(F32)).astype(BF16)
        both = jnp.concatenate([first, second], axis=1)
        product = jnp.zeros((width, 2 * LANE), F32)
        for index, ref in enumerate((normed, other_ref)):
            rows_of = slice(index * total // 2, (index + 1) * total // 2)
            product += lax.dot_general(
                ref[...], both[rows_of], (((0,), (0,)), ((), ())), preferred_element_type=F32
            )
        product = (product[:, :LANE] + product[:, LANE:]).astype(BF16)
        out_ref[:, EDGE * (part + 1) : EDGE * (part + 2), :] = product.reshape(peers, EDGE, LANE)
    sends[1].start()
    for send in sends:
        send.wait()


def share_kernel(arrived_ref, copies_ref):
    peers = arrived_ref.shape[0]
    for part in range(MEMBERS):
        for half in range(HALVES):
            total = jnp.zeros((EDGE, LANE), F32)
            for group in range(peers // MEMBERS):
                total += arrived_ref[
                    group * MEMBERS + part, EDGE * (half + 1) : EDGE * (half + 2), :
                ].astype(F32)
            first = (part * HALVES + half) * LANE
            for copy in range(copies_ref.shape[0]):
                copies_ref[copy, :, first : first + LANE] = total.astype(BF16)


def frame_kernel(
    arrived_ref, toks_ref, kernel_far, back_ref, ahead_ref, out_ref,
    shifted, taps, low, high, kernel_here, sem, spread,
):
    frame_count = out_ref.shape[0]
    rows = shifted.shape[1]
    columns = 2 * arrived_ref.shape[0]
    spread[...] = arrived_ref[:, :EDGE, :].astype(F32).reshape(columns * ROWS, LANE)
    chosen = down_rows(toks_ref[...] & columns - 1, rows)
    onehot = chosen == lax.broadcasted_iota(I32, (rows, columns), 1).astype(F32)
    onehot = jnp.where(onehot, 1.0, 0.0).astype(BF16)
    for part in range(ROWS):
        shifted[0, :, part * LANE : (part + 1) * LANE] = jnp.dot(
            onehot,
            spread[pl.ds(part, columns, stride=ROWS), :].astype(BF16),
            preferred_element_type=F32,
        )
    low[...] = down_rows(back_ref[...], frame_count)
    high[...] = down_rows(ahead_ref[...], frame_count)
    prepare(shifted, taps, kernel_far, kernel_here, sem)
    convolve(shifted, taps, low, high, 1, EDGE, out_ref, frame_count // EDGE)


SMALL, LARGE = pl.BlockSpec(memory_space=pltpu.SMEM), pl.BlockSpec(memory_space=pltpu.VMEM)
FAR = pl.BlockSpec(memory_space=pltpu.HBM)


def far(array):
    return pltpu.with_memory_space_constraint(array, pltpu.HBM)


def call(kernel, outs, scratch, flops, moved, ins=None, mib=16, to=None):
    options = {} if ins is None else {"in_specs": ins}
    if to is not None:
        options["out_specs"] = to
    return pl.pallas_call(
        kernel,
        out_shape=outs,
        scratch_shapes=scratch,
        compiler_params=pltpu.CompilerParams(vmem_limit_bytes=mib * 1024 * 1024),
        cost_estimate=pl.CostEstimate(flops=flops, bytes_accessed=moved, transcendentals=0),
        **options,
    )


def all_to_all(blocks, axis):
    return lax.all_to_all(blocks, axis, split_axis=0, concat_axis=0, tiled=True)


def body(tokens, text_weight, conv_kernel, frame_token, seg_before, seg_after, cotangent):
    peers = lax.axis_size("seq")
    shards = lax.axis_size("dp")
    rank = lax.axis_index("seq")
    slots, block_rows, width = tokens.shape[1], tokens.shape[3], tokens.shape[4]
    half_span = conv_kernel.shape[0] // 2
    frame_count = cotangent.shape[1]
    own_rows = slots * block_rows
    cot = cotangent[0]
    rank_word = rank[None]

    rim = jax.ShapeDtypeStruct((LEAD, width), BF16)
    line = jax.ShapeDtypeStruct((1, frame_count), I32)
    blocks = tokens.reshape(slots, block_rows, width)
    given = [far(array) for array in (cot, frame_token, seg_before, seg_after, blocks)]
    tail, cot, toks, back, ahead, normed = call(
        rim_kernel,
        [rim, jax.ShapeDtypeStruct(cot.shape, BF16), line, line, line]
        + [jax.ShapeDtypeStruct((own_rows, width), BF16)],
        [
            pltpu.VMEM((ROWS, width), F32),
            pltpu.VMEM(blocks.shape, BF16),
            pltpu.SemaphoreType.DMA((len(given),)),
        ],
        8 * EDGE * width,
        4 * frame_count * width,
        [FAR] * len(given),
        mib=4,
    )(*given)
    before = lax.ppermute(tail, "seq", [(i, i + 1) for i in range(peers - 1)])
    def hop(rows, count):
        path = [(i, i // MEMBERS * MEMBERS + (i + 2 * count) % MEMBERS) for i in range(peers)]
        return lax.ppermute(rows, "seq", path)

    near = [hop(normed, 1), hop(normed, 2)]

    def scratch(rows, frames):
        return [
            pltpu.VMEM((ROWS, rows, width), F32),
            pltpu.VMEM((conv_kernel.shape[0], ROWS, width), F32),
            pltpu.VMEM((frames, LANE), F32),
            pltpu.VMEM((frames, LANE), F32),
            pltpu.VMEM(conv_kernel.shape, BF16),
            pltpu.SemaphoreType.DMA,
        ]

    work = 12 * conv_kernel.shape[0] * frame_count * width
    packed = call(
        grad_kernel,
        jax.ShapeDtypeStruct((peers, FOLD, (FOLD + 1) * LANE), BF16),
        scratch(LEAD + frame_count + EDGE, frame_count + EDGE)
        + [pltpu.VMEM((frame_count + EDGE, width), BF16)],
        work,
        4 * frame_count * width,
        [SMALL] + [LARGE] * 2 + [FAR] + [LARGE] * 3,
    )(rank_word, cot, before, far(conv_kernel), back, ahead, toks)
    later, packed = lax.optimization_barrier((normed, packed))
    text_rows = call(
        text_kernel,
        jax.ShapeDtypeStruct((own_rows, width), BF16),
        [],
        2 * own_rows * width * width,
        24 * width * width,
        mib=8,
    )(later, text_weight)
    pieces = [normed, near[0], near[1], hop(later, 3)]
    same, text_rows = lax.optimization_barrier((jnp.concatenate(pieces), text_rows))
    other = lax.ppermute(same, "seq", [(i, i ^ 1) for i in range(peers)])

    returned = all_to_all(packed, "seq")

    def joined(upper, lower):
        return (upper.astype(I32) << SPLIT_BITS) + lower.astype(I32)

    ends = slice(frame_count - half_span, frame_count)
    none = jnp.zeros((1,), I32)
    ahead_notes = lax.dynamic_index_in_dim(
        returned[:, :, FOLD * LANE : FOLD * LANE + half_span], (rank + 1) % peers, keepdims=False
    )
    all_toks = jnp.concatenate(
        [
            none,
            joined(before[0, ends], before[0, LOW_AT:][ends]),
            toks[0],
            joined(ahead_notes[2], ahead_notes[3]),
            none,
        ]
    )[None]
    product = call(
        lambda *refs: product_kernel(
            *refs, slots=slots, block_rows=block_rows, frame_count=frame_count
        ),
        jax.ShapeDtypeStruct((peers, EDGE * (1 + HALVES), LANE), BF16),
        [
            pltpu.VMEM((peers * FOLD, LANE), F32),
            pltpu.VMEM((MEMBERS // 2 * own_rows, width), BF16),
            pltpu.VMEM((peers * EDGE, LANE), F32),
            pltpu.SemaphoreType.DMA((4,)),
            pltpu.VMEM((peers, EDGE * (1 + HALVES), LANE), BF16),
            pltpu.SemaphoreType.DMA((2,)),
        ],
        4 * MEMBERS * own_rows * width * LANE * HALVES,
        4 * MEMBERS * own_rows * width,
        [SMALL] + [LARGE] * 2 + [FAR, LARGE],
        24,
        FAR,
    )(rank_word, returned, text_rows, far(same), other)
    arrived = all_to_all(product, "seq")

    copies = call(
        share_kernel,
        jax.ShapeDtypeStruct((shards, width // peers, width), BF16),
        [],
        peers * EDGE * HALVES * LANE,
        peers * EDGE * HALVES * LANE,
    )(arrived)
    shares = all_to_all(copies, "dp")
    summed = jnp.sum(shares.astype(F32), axis=0)

    frames_out = call(
        frame_kernel,
        jax.ShapeDtypeStruct((frame_count, width), BF16),
        scratch(frame_count + 2 * EDGE, frame_count) + [pltpu.VMEM((peers * EDGE, LANE), F32)],
        work,
        4 * frame_count * width,
        [LARGE] * 2 + [FAR] + [LARGE] * 2,
    )(arrived, all_toks, far(conv_kernel), back, ahead)
    return (frames_out[None], summed)


def solution(mesh):
    in_specs = (
        P("dp", None, "seq", None, None),
        P(),
        P(),
        P("dp", "seq"),
        P("dp", "seq"),
        P("dp", "seq"),
        P("dp", "seq", None),
    )
    out_specs = (P("dp", "seq", None), P("seq", None))
    return jax.shard_map(body, mesh=mesh, in_specs=in_specs, out_specs=out_specs, check_vma=False)
```
